256 devices in a mesh: row: 4 (over z_hi), col: 8 (over z_lo, y), depth: 8 (over x, core).
Axes of the slice: x: 4, y: 4, z: 8 (z_hi: 4, z_lo: 2; z = z_hi * 2 + z_lo), core: 2. Of those that a mesh axis runs over, the one named last changes fastest.
Arguments:
- tokens: bfloat16 [6144, 8192], P('col', 'depth'), may hold values from -6 to 6
- weight: bfloat16 [4096, 3, 8192], P(('row', 'col'), None, 'depth'), may hold values from -0.0625 to 0.0625
- taps: float32 [7, 256], P(None, 'row'), may hold values from -3 to 3
- upstream: bfloat16 [6144, 4096], P(('col', 'depth'), 'row'), may hold values from -6 to 6
Outputs:
- output: bfloat16 [6144, 4096], P(('col', 'depth'), 'row')
- grad_tokens: bfloat16 [6144, 8192], P('col', 'depth')
- grad_weight: float32 [4096, 3, 8192], P(('row', 'col'), None, 'depth')
- grad_taps: float32 [7, 256], P(None, 'row')
The draws below stay inside these ranges and needn't reach their ends.
All inputs are finite; a program needn't handle non-finite values.
Results may differ from the reference program's by a relative error of at most 0.034.
Values may be sent and summed in bfloat16 or wider, within the bound.
A program may use at most 128 MiB of HBM per device.

```python
import jax
import jax.numpy as jnp
from jax import lax

D = 8192
C = 4096
GROUP = 16
KT = 7
GROUPS = 256
GROUP_TOK = 768
TOKENS = 6144
N_COL = 8


def block_scale(key, shape, cuts, least, high):
    loudness = 1.0
    for axis_at, parts in cuts:
        draws = jax.random.uniform(jax.random.fold_in(jax.random.fold_in(key, 6), axis_at), (parts,), jnp.float32, least / len(cuts), high / len(cuts))
        loudness = loudness * jnp.repeat(jnp.exp(draws), shape[axis_at] // parts).reshape((-1,) + (1,) * (len(shape) - 1 - axis_at))
    return loudness


def centred(key, dims, scale, bound, shards=(), dtype=jnp.bfloat16):
    loudness = block_scale(key, dims, shards, -0.22, 0.18) if shards else 1.0
    result = jax.random.normal(key, dims, jnp.float32) * scale * loudness
    return jnp.minimum(jnp.maximum(result, -bound), bound).astype(dtype)


def setup_inputs(seed: int = 0) -> dict:
    seeds = jax.random.split(jax.random.key(seed), 5)
    return {
        "tokens": centred(seeds[0], (TOKENS, D), 1.0, 6.0, ((0, 8), (1, 8))),
        "weight": centred(seeds[1], (C, 3, D), D ** -0.5, 0.0625, ((0, 32), (2, 8))),
        "taps": centred(seeds[2], (KT, GROUPS), 0.5, 3.0, ((1, 4),), jnp.float32),
        "upstream": centred(seeds[3], (TOKENS, C), 1.0, 6.0, ((0, 64), (1, 4))),
    }


def causal_filter(padded, spread, length):
    total = jnp.zeros((length, padded.shape[1]), jnp.float32)
    for offset in range(KT):
        first_row = KT - 1 - offset
        total = total + spread[offset] * padded[first_row:first_row + length]
    return total


def reference(tokens, weight, taps, upstream):
    flat_weight = jnp.transpose(weight, (1, 0, 2)).reshape(3 * C, D)
    projected = jnp.dot(tokens, flat_weight.T, preferred_element_type=jnp.float32)
    rounded = lax.optimization_barrier(projected.astype(jnp.bfloat16)).astype(jnp.float32)
    rounded = rounded.reshape(TOKENS, 3, C)
    query_part = rounded[:, 0, :]
    key_part = rounded[:, 1, :]
    value_part = rounded[:, 2, :]
    mixed = key_part * value_part
    spread = jnp.repeat(taps.astype(jnp.float32), GROUP, axis=1)
    padded = jnp.concatenate([jnp.zeros((KT - 1, C), jnp.float32), mixed], 0)
    filtered = causal_filter(padded, spread, TOKENS)
    output = (query_part * filtered).astype(jnp.bfloat16)
    upstream_f = upstream.astype(jnp.float32)
    grad_query = upstream_f * filtered
    grad_filtered = upstream_f * query_part
    padded_grad = jnp.concatenate([grad_filtered, jnp.zeros((KT - 1, C), jnp.float32)], 0)
    grad_mixed = jnp.zeros((TOKENS, C), jnp.float32)
    for offset in range(KT):
        grad_mixed = grad_mixed + spread[offset] * padded_grad[offset:offset + TOKENS]
    grad_key = grad_mixed * value_part
    grad_value = grad_mixed * key_part
    grad_proj = jnp.stack([grad_query, grad_key, grad_value], axis=1).astype(jnp.bfloat16)
    tap_rows = []
    for offset in range(KT):
        first_row = KT - 1 - offset
        summed = jnp.sum(grad_filtered * padded[first_row:first_row + TOKENS], axis=0)
        tap_rows.append(summed.reshape(GROUPS, GROUP).sum(axis=1))
    grad_taps = jnp.stack(tap_rows, 0)
    flat_grad = grad_proj.reshape(TOKENS, 3 * C)
    grad_flat_w = jnp.zeros((3 * C, D), jnp.float32)
    for block in range(N_COL):
        grad_rows = flat_grad[block * GROUP_TOK:(block + 1) * GROUP_TOK]
        token_rows = tokens[block * GROUP_TOK:(block + 1) * GROUP_TOK]
        partial_w = jnp.dot(grad_rows.T, token_rows, preferred_element_type=jnp.float32)
        partial_w = lax.optimization_barrier(partial_w.astype(jnp.bfloat16)).astype(jnp.float32)
        grad_flat_w = grad_flat_w + partial_w
    grad_weight = jnp.transpose(grad_flat_w.reshape(3, C, D), (1, 0, 2))
    grad_tokens = jnp.dot(flat_grad, flat_weight, preferred_element_type=jnp.float32).astype(jnp.bfloat16)
    return output, grad_tokens, grad_weight, grad_taps
```

```python
import jax
import jax.numpy as jnp
from jax import lax
from jax.experimental import pallas as pl
from jax.experimental.pallas import tpu as pltpu
from jax.sharding import PartitionSpec as P

MESH = pl.DeviceIdType.MESH
F32 = jnp.float32
BF16 = jnp.bfloat16
GROUP = 16
KT = 7
TOK = 768
ROWS = 96
CH = 128
SH = 3 * CH
DL = 1024
HALF = 512


def fma_dot(a, b, dims):
    return lax.dot_general(a, b, (dims, ((), ())), preferred_element_type=F32)


def kernel(
    tok_in, w_in, taps_ref, up_in,
    out_ref, gt_ref, gw_ref, ts_ref,
    T, W, U, PP, SB, S, R2, RM, RP, QKV, MX, GF, HM, HG, OB, G,
    TS, TR, TC, TY, TZ, PW, DR, DS, ES, ER, EO,
    l_sem, w_s, w_r, t_s, t_r, u_s, u_r, b_s, b_r, h_s, h_r, c_s, c_r,
    tr_s, tr_r, ty_s, ty_r, tz_s, tz_r, o_s, o_r, d_s, d_r, e_s, e_r, g_s, g_r,
):
    r, c, d = lax.axis_index("row"), lax.axis_index("col"), lax.axis_index("depth")
    zl, y, x, k = c // 4, c % 4, d // 2, d % 2
    z = 2 * r + zl

    def znb(delta):
        other = (z + delta + 8) % 8
        return (other // 2, (other % 2) * 4 + y, d)

    def ynb(delta):
        return (r, zl * 4 + (y + delta + 4) % 4, d)

    def xnb(delta):
        return (r, c, ((x + delta + 4) % 4) * 2 + k)

    def dnb(delta):
        return (r, c, (d + delta + 8) % 8)

    sib = (r, c, x * 2 + 1 - k)
    pair = (r, (1 - zl) * 4 + y, d)
    wraps_up = jnp.where(d == 7, 1, 0)
    wraps_down = jnp.where(d == 0, 1, 0)
    following = (r, zl * 4 + (y + wraps_up) % 4, (d + 1) % 8)
    previous = (r, zl * 4 + (y + 4 - wraps_down) % 4, (d + 7) % 8)

    def remote(src, dst, ssem, rsem, to):
        return pltpu.make_async_remote_copy(
            src_ref=src, dst_ref=dst, send_sem=ssem, recv_sem=rsem, device_id=to, device_id_type=MESH
        )

    sends = []

    def send(src, dst, ssem, rsem, to):
        copy = remote(src, dst, ssem, rsem, to)
        copy.start()
        sends.append(copy)

    def arrived(dst, rsem):
        remote(dst, dst, l_sem.at[0], rsem, sib).wait_recv()

    barrier = pltpu.get_barrier_semaphore()
    partners = [dnb(delta) for delta in range(1, 8)]
    partners += [ynb(delta) for delta in range(1, 4)]
    partners += [znb(delta) for delta in (1, -1, 2, -2)]
    partners += [following, previous]
    for partner in partners:
        pl.semaphore_signal(barrier, inc=1, device_id=partner, device_id_type=MESH)
    locals_ = [
        pltpu.make_async_copy(tok_in, T.at[0], l_sem.at[1]),
        pltpu.make_async_copy(w_in, W.at[y], l_sem.at[2]),
        pltpu.make_async_copy(
            up_in.at[:, pl.ds(pl.multiple_of(zl * HALF, HALF), HALF)], U.at[0], l_sem.at[3]
        ),
    ]
    for copy in locals_:
        copy.start()
    pl.semaphore_wait(barrier, len(partners))

    for first, way, side in ((0, 1, 0), (1, -1, 1)):
        for part in (first, 1 - first):
            send(w_in.at[part], W.at[y, part], w_s.at[side, part], w_r.at[side, part], ynb(way))
    send(tok_in.at[pl.ds(0, 384)], T.at[1, pl.ds(0, 384)], t_s.at[0], t_r.at[0], znb(-1))
    send(tok_in.at[pl.ds(384, 384)], T.at[1, pl.ds(384, 384)], t_s.at[1], t_r.at[1], znb(1))
    send(
        up_in.at[:, pl.ds(pl.multiple_of((1 - zl) * HALF, HALF), HALF)],
        U.at[1], u_s.at[0], u_r.at[0], pair,
    )
    for copy in locals_:
        copy.wait()

    def unit(u):
        i = u // 2
        return u % 2, (y + (i * (7 - i)) // 2) % 4

    def to_sibling(g, j):
        return remote(PP.at[g, j, :, 1 - k], SB.at[g, j], b_s.at[0, g, j], b_r.at[0, g, j], sib)

    def far(g, j):
        way = 1 - 2 * g
        return remote(S.at[g, j, (x + 2) % 4], R2.at[g, j], b_s.at[1, g, j], b_r.at[1, g, j], xnb(way))

    def back(g, j):
        way = 1 - 2 * g
        return remote(
            S.at[g, j, (x - way + 4) % 4], RM.at[g, j], b_s.at[2, g, j], b_r.at[2, g, j], xnb(-way)
        )

    def near(g, j):
        way = 1 - 2 * g
        return remote(
            S.at[g, j, (x + way + 4) % 4], RP.at[g, j], b_s.at[3, g, j], b_r.at[3, g, j], xnb(way)
        )

    def project(u):
        g, j = unit(u)
        part = fma_dot(T[g], W[j].reshape(SH, DL), ((1,), (1,)))
        PP[g, j] = part.astype(BF16).reshape(4, 2, ROWS, SH)
        to_sibling(g, j).start()

    def chip_sum(u):
        g, j = unit(u)
        to_sibling(g, j).wait_recv()
        for at in range(4):
            S[g, j, at] = (PP[g, j, at, k].astype(F32) + SB[g, j, at].astype(F32)).astype(BF16)
        far(g, j).start()
        back(g, j).start()

    def relay(u):
        g, j = unit(u)
        far(g, j).wait_recv()
        at = (x + 1 - 2 * g + 4) % 4
        S[g, j, at] = (S[g, j, at].astype(F32) + R2[g, j].astype(F32)).astype(BF16)
        near(g, j).start()

    def project_step(u, carry):
        @pl.when(u == 1)
        def _():
            chip_sum(0)
            arrived(W.at[(y + 3) % 4, 0], w_r.at[0, 0])
            remote(
                W.at[(y + 3) % 4, 0], W.at[(y + 3) % 4, 0], w_s.at[2, 0], w_r.at[2, 0], ynb(1)
            ).start()
            arrived(W.at[(y + 1) % 4, 1], w_r.at[1, 1])
            remote(
                W.at[(y + 1) % 4, 1], W.at[(y + 1) % 4, 1], w_s.at[2, 1], w_r.at[2, 1], ynb(-1)
            ).start()
            arrived(T.at[1, pl.ds(0, 384)], t_r.at[0])
            arrived(T.at[1, pl.ds(384, 384)], t_r.at[1])

        @pl.when(u == 2)
        def _():
            arrived(W.at[(y + 3) % 4, 1], w_r.at[0, 1])

        @pl.when(u == 4)
        def _():
            arrived(W.at[(y + 1) % 4, 0], w_r.at[1, 0])

        @pl.when(u == 6)
        def _():
            chip_sum(5)
            lax.fori_loop(0, 6, lambda v, unused: (relay(v), unused)[1], 0)
            arrived(W.at[(y + 2) % 4, 0], w_r.at[2, 0])
            arrived(W.at[(y + 2) % 4, 1], w_r.at[2, 1])

        project(u)

        @pl.when((u >= 2) & (u != 6))
        def _():
            chip_sum(u - 1)

        return carry

    lax.fori_loop(0, 8, project_step, 0)
    chip_sum(7)
    lax.fori_loop(6, 8, lambda v, unused: (relay(v), unused)[1], 0)
    arrived(U.at[1], u_r.at[0])

    def mixed_rows(j):
        return remote(MX.at[j, :, pl.ds(ROWS, 8)], HM.at[j], h_s.at[0, j], h_r.at[0, j], following)

    def grad_rows(j):
        return remote(GF.at[j, :, pl.ds(0, 8)], HG.at[j], h_s.at[1, j], h_r.at[1, j], previous)

    def total_step(i, carry):
        for g in range(2):
            _, j = unit(2 * i)
            back(g, j).wait_recv()
            near(g, j).wait_recv()
            total = S[g, j, x].astype(F32) + RM[g, j].astype(F32) + RP[g, j].astype(F32)
            total = total.astype(BF16).astype(F32)
            up = U[g, :, pl.ds(pl.multiple_of(j * CH, CH), CH)].astype(F32)
            QKV[g, j] = total
            MX[j, g, pl.ds(8, ROWS)] = total[:, CH : 2 * CH] * total[:, 2 * CH :]
            GF[j, g, pl.ds(0, ROWS)] = up * total[:, :CH]
        mixed_rows(j).start()
        grad_rows(j).start()
        return carry

    lax.fori_loop(0, 4, total_step, 0)

    def own_piece(g, j, way, at):
        return remote(
            G.at[g, j, x, k], G.at[g, j, x, k], c_s.at[at, g, j], c_r.at[at, g, j], xnb(way)
        )

    def relayed_piece(g, j):
        way = 1 - 2 * g
        at = (x - way + 4) % 4
        return remote(G.at[g, j, at, k], G.at[g, j, at, k], c_s.at[2, g, j], c_r.at[2, g, j], xnb(way))

    def to_sibling_back(g, j):
        return remote(G.at[g, j, :, k], G.at[g, j, :, k], c_s.at[3, g, j], c_r.at[3, g, j], sib)

    at_start = (y == 0) & (d == 0)
    at_end = (y == 3) & (d == 7)

    def halo_weights(edge, g, first):
        group = zl if g == 0 else 1 - zl
        same = jnp.where(edge, 0.0, 1.0)
        swapped = jnp.where(edge & (group == (1 if first else 0)), 1.0, 0.0)
        return same, swapped

    def filter_step(i, carry):
        _, j = unit(2 * i)
        mixed_rows(j).wait_recv()
        grad_rows(j).wait_recv()
        taps = taps_ref[zl * 4 + j]
        tap_sums = [None] * KT
        for g in range(2):
            same, swapped = halo_weights(at_start, g, True)
            MX[j, g, pl.ds(0, 8)] = HM[j, g] * same + HM[j, 1 - g] * swapped
            same, swapped = halo_weights(at_end, g, False)
            GF[j, g, pl.ds(ROWS, 8)] = HG[j, g] * same + HG[j, 1 - g] * swapped
            query = QKV[g, j, :, :CH]
            up = U[g, :, pl.ds(pl.multiple_of(j * CH, CH), CH)].astype(F32)
            grad = GF[j, g, pl.ds(0, ROWS)]
            filtered = jnp.zeros((ROWS, CH), F32)
            grad_mixed = jnp.zeros((ROWS, CH), F32)
            for o in range(KT):
                shifted = MX[j, g, pl.ds(8 - o, ROWS)]
                tap = taps[o : o + 1]
                filtered = filtered + tap * shifted
                grad_mixed = grad_mixed + tap * GF[j, g, pl.ds(o, ROWS)]
                summed = jnp.sum(grad * shifted, axis=0, keepdims=True)
                tap_sums[o] = summed if g == 0 else tap_sums[o] + summed
            gated = (query * filtered).astype(BF16)
            if g == 0:
                out_ref[:, pl.ds(pl.multiple_of((zl * 4 + j) * CH, CH), CH)] = gated
            else:
                OB[:, pl.ds(pl.multiple_of(j * CH, CH), CH)] = gated
            G[g, j, x, k, :, pl.ds(0, CH)] = (up * filtered).astype(BF16)
            G[g, j, x, k, :, pl.ds(CH, CH)] = (grad_mixed * QKV[g, j, :, 2 * CH :]).astype(BF16)
            G[g, j, x, k, :, pl.ds(2 * CH, CH)] = (grad_mixed * QKV[g, j, :, CH : 2 * CH]).astype(BF16)
            own_piece(g, j, 1, 0).start()
            own_piece(g, j, -1, 1).start()
        TS[j] = jnp.concatenate(tap_sums + [jnp.zeros((1, CH), F32)], axis=0)
        return carry

    lax.fori_loop(0, 4, filter_step, 0)

    def relay_piece_step(i, carry):
        _, j = unit(2 * i)
        own_piece(0, j, 1, 0).wait_recv()
        relayed_piece(0, j).start()
        own_piece(1, j, -1, 1).wait_recv()
        relayed_piece(1, j).start()
        return carry

    lax.fori_loop(0, 4, relay_piece_step, 0)

    def sibling_piece_step(i, carry):
        _, j = unit(2 * i)
        own_piece(0, j, -1, 1).wait_recv()
        own_piece(1, j, 1, 0).wait_recv()
        for g in range(2):
            relayed_piece(g, j).wait_recv()
            to_sibling_back(g, j).start()
        return carry

    lax.fori_loop(0, 4, sibling_piece_step, 0)
    send(
        OB, out_ref.at[:, pl.ds(pl.multiple_of(zl * HALF, HALF), HALF)], o_s.at[0], o_r.at[0], pair
    )
    for delta in range(1, 8):
        send(TS, TR.at[d], tr_s.at[delta], tr_r.at[d], dnb(delta))

    def gathered_step(i, carry):
        _, j = unit(2 * i)
        for g in range(2):
            to_sibling_back(g, j).wait_recv()
        return carry

    lax.fori_loop(0, 4, gathered_step, 0)

    def chunk(delta, side):
        group = abs(delta) % 2
        at = ((z + delta + 8) % 8) // 2
        total = None
        for j in range(4):
            rows = G[group, j, at].reshape(2 * ROWS, SH)
            columns = W[j, :, :, side * HALF : (side + 1) * HALF].reshape(SH, HALF)
            term = fma_dot(rows, columns, ((1,), (0,)))
            total = term if total is None else total + term
        return total

    def landed_chunk(way, steps, side):
        arrived(ER.at[way, steps, side], e_r.at[way, steps, side])
        return ER[way, steps, side].astype(F32)

    def send_chunk(way, steps, side, value):
        ES[way, steps, side] = value.astype(BF16)
        send(
            ES.at[way, steps, side], ER.at[way, steps, side],
            e_s.at[way, steps, side], e_r.at[way, steps, side], znb(1 - 2 * way),
        )

    def shard_grad(delta):
        j = (y + delta + 4) % 4
        total = None
        for g in range(2):
            term = fma_dot(G[g, j].reshape(TOK, SH), T[g], ((0,), (0,)))
            total = term if total is None else total + term
        return total

    def send_grad(way, kind, value):
        DS[way, kind] = value.astype(BF16)
        send(DS.at[way, kind], DR.at[way, kind], d_s.at[way, kind], d_r.at[way, kind], ynb(1 - 2 * way))

    def landed_grad(way, kind):
        arrived(DR.at[way, kind], d_r.at[way, kind])
        return DR[way, kind].astype(F32)

    cut = SH // 2
    send_chunk(0, 4, 0, chunk(4, 0))
    send_chunk(1, 4, 1, chunk(-4, 1))
    send_chunk(0, 3, 1, chunk(3, 1))
    send_chunk(1, 3, 0, chunk(-3, 0))
    part = shard_grad(2)
    send_grad(0, 0, part[:cut])
    send_grad(1, 0, part[cut:])
    send_chunk(0, 3, 0, chunk(3, 0) + landed_chunk(0, 4, 0))
    send_chunk(1, 3, 1, chunk(-3, 1) + landed_chunk(1, 4, 1))
    part = shard_grad(1)
    send_grad(0, 1, part[cut:])
    PW[0] = part[:cut]
    part = shard_grad(-1)
    send_grad(1, 1, part[:cut])
    PW[1] = part[cut:]
    send_chunk(0, 2, 1, chunk(2, 1) + landed_chunk(0, 3, 1))
    send_chunk(1, 2, 0, chunk(-2, 0) + landed_chunk(1, 3, 0))
    send_grad(0, 2, PW[0] + landed_grad(0, 0))
    send_grad(1, 2, PW[1] + landed_grad(1, 0))
    send_chunk(0, 2, 0, chunk(2, 0) + landed_chunk(0, 3, 0))
    send_chunk(1, 2, 1, chunk(-2, 1) + landed_chunk(1, 3, 1))

    TR[d] = TS[...]
    for delta in range(1, 8):
        source = (d + delta) % 8
        arrived(TR.at[source], tr_r.at[source])
    total = TR[0]
    for at in range(1, 8):
        total = total + TR[at]
    TC[...] = total
    TY[y] = total
    for delta in range(1, 4):
        send(TC, TY.at[y], ty_s.at[delta], ty_r.at[y], ynb(delta))

    send_chunk(0, 1, 1, chunk(1, 1) + landed_chunk(0, 2, 1))
    send_chunk(1, 1, 0, chunk(-1, 0) + landed_chunk(1, 2, 0))
    part = shard_grad(0)
    send_chunk(0, 1, 0, chunk(1, 0) + landed_chunk(0, 2, 0))
    send_chunk(1, 1, 1, chunk(-1, 1) + landed_chunk(1, 2, 1))
    gw_ref[...] = part

    for delta in range(1, 4):
        source = (y + delta) % 4
        arrived(TY.at[source], ty_r.at[source])
    total = TY[0]
    for at in range(1, 4):
        total = total + TY[at]
    TZ[...] = total
    ts_ref[zl] = total
    send(TZ, ts_ref.at[zl], tz_s.at[0], tz_r.at[0], pair)

    EO[1] = chunk(0, 1)
    EO[0] = chunk(0, 0)
    own_rows = pl.multiple_of(r * 2 * ROWS, 2 * ROWS)
    for side in (1, 0):
        columns = pl.ds(side * HALF, HALF)
        final = EO[side] + landed_chunk(0, 1, side) + landed_chunk(1, 1, side)
        gt_ref[pl.ds(own_rows, 2 * ROWS), columns] = final.astype(BF16)

    def final_rows(row, part):
        at = pl.multiple_of(((row + 4) % 4) * 2 * ROWS + part * ROWS, ROWS)
        return gt_ref.at[pl.ds(at, ROWS)]

    for part, way in ((0, 0), (1, 1), (1, 0), (0, 1)):
        rows = final_rows(r, part)
        send(rows, rows, g_s.at[way, part], g_r.at[way, part], znb(2 - 4 * way))
    for way in range(2):
        rows = final_rows(r - 1 + 2 * way, way)
        arrived(rows, g_r.at[way, way])
        send(rows, rows, g_s.at[2, way], g_r.at[2, way], znb(2 - 4 * way))

    for side in range(2):
        near_rows = pl.ds((1 - side) * cut, cut)
        mine = gw_ref[pl.ds(side * cut, cut)]
        if side == 0:
            mine = mine + landed_grad(0, 2) + landed_grad(1, 1)
        else:
            mine = mine + landed_grad(0, 1) + landed_grad(1, 2)
        gw_ref[pl.ds(side * cut, cut)] = mine

    arrived(final_rows(r - 1, 1), g_r.at[0, 1])
    arrived(final_rows(r + 1, 0), g_r.at[1, 0])
    arrived(final_rows(r + 2, 0), g_r.at[2, 0])
    arrived(final_rows(r + 2, 1), g_r.at[2, 1])
    arrived(ts_ref.at[1 - zl], tz_r.at[0])
    arrived(out_ref.at[:, pl.ds(pl.multiple_of((1 - zl) * HALF, HALF), HALF)], o_r.at[0])

    for copy in sends:
        copy.wait_send()
    for part, shard, way in ((0, 3, 1), (1, 1, -1)):
        rows = W.at[(y + shard) % 4, part]
        remote(rows, rows, w_s.at[2, part], w_r.at[2, part], ynb(way)).wait_send()

    def sent_step(j, carry):
        mixed_rows(j).wait_send()
        grad_rows(j).wait_send()
        for g in range(2):
            for copy in (to_sibling(g, j), far(g, j), back(g, j), near(g, j)):
                copy.wait_send()
            for copy in (
                own_piece(g, j, 1, 0), own_piece(g, j, -1, 1), relayed_piece(g, j), to_sibling_back(g, j)
            ):
                copy.wait_send()
        return carry

    lax.fori_loop(0, 4, sent_step, 0)


def on_device(tokens, weight, taps, upstream):
    shard = weight.transpose(1, 0, 2).reshape(2, SH // 2, DL)
    spread = jnp.repeat(taps, GROUP, axis=1)
    spread = jnp.concatenate([spread, jnp.zeros((1, spread.shape[1]), F32)], 0)
    spread = spread.reshape(8, 8, CH).transpose(1, 0, 2)
    vmem = pl.BlockSpec(memory_space=pltpu.VMEM)
    anywhere = pl.BlockSpec(memory_space=pl.ANY)
    dma = pltpu.SemaphoreType.DMA
    scratch = [
        pltpu.VMEM((2, TOK, DL), BF16),
        pltpu.VMEM((4, 2, SH // 2, DL), BF16),
        pltpu.VMEM((2, ROWS, HALF), BF16),
        pltpu.VMEM((2, 4, 4, 2, ROWS, SH), BF16),
        pltpu.VMEM((2, 4, 4, ROWS, SH), BF16),
        pltpu.VMEM((2, 4, 4, ROWS, SH), BF16),
        pltpu.VMEM((2, 4, ROWS, SH), BF16),
        pltpu.VMEM((2, 4, ROWS, SH), BF16),
        pltpu.VMEM((2, 4, ROWS, SH), BF16),
        pltpu.VMEM((2, 4, ROWS, SH), F32),
        pltpu.VMEM((4, 2, ROWS + 8, CH), F32),
        pltpu.VMEM((4, 2, ROWS + 8, CH), F32),
        pltpu.VMEM((4, 2, 8, CH), F32),
        pltpu.VMEM((4, 2, 8, CH), F32),
        pltpu.VMEM((ROWS, HALF), BF16),
        pltpu.VMEM((2, 4, 4, 2, ROWS, SH), BF16),
        pltpu.VMEM((4, 8, CH), F32),
        pltpu.VMEM((8, 4, 8, CH), F32),
        pltpu.VMEM((4, 8, CH), F32),
        pltpu.VMEM((4, 4, 8, CH), F32),
        pltpu.VMEM((4, 8, CH), F32),
        pltpu.VMEM((2, SH // 2, DL), F32),
        pltpu.VMEM((2, 3, SH // 2, DL), BF16),
        pltpu.VMEM((2, 3, SH // 2, DL), BF16),
        pltpu.VMEM((2, 5, 2, 2 * ROWS, HALF), BF16),
        pltpu.VMEM((2, 5, 2, 2 * ROWS, HALF), BF16),
        pltpu.VMEM((2, 2 * ROWS, HALF), F32),
        dma((4,)),
        dma((3, 2)), dma((3, 2)),
        dma((2,)), dma((2,)),
        dma((1,)), dma((1,)),
        dma((4, 2, 4)), dma((4, 2, 4)),
        dma((2, 4)), dma((2, 4)),
        dma((4, 2, 4)), dma((4, 2, 4)),
        dma((8,)), dma((8,)),
        dma((4,)), dma((4,)),
        dma((1,)), dma((1,)),
        dma((1,)), dma((1,)),
        dma((2, 3)), dma((2, 3)),
        dma((2, 5, 2)), dma((2, 5, 2)),
        dma((3, 2)), dma((3, 2)),
    ]
    output, grad_tokens, grad_weight, sums = pl.pallas_call(
        kernel,
        out_shape=(
            jax.ShapeDtypeStruct((ROWS, 2 * HALF), BF16),
            jax.ShapeDtypeStruct((TOK, DL), BF16),
            jax.ShapeDtypeStruct((SH, DL), F32),
            jax.ShapeDtypeStruct((2, 4, 8, CH), F32),
        ),
        in_specs=[anywhere, anywhere, vmem, anywhere],
        out_specs=(vmem, vmem, vmem, vmem),
        scratch_shapes=scratch,
        compiler_params=pltpu.CompilerParams(
            collective_id=0, has_side_effects=True, vmem_limit_bytes=58 * 1024 * 1024
        ),
        cost_estimate=pl.CostEstimate(
            flops=6 * TOK * DL * 8 * SH, bytes_accessed=8 * 1024 * 1024, transcendentals=0
        ),
    )(tokens, shard, spread, upstream)
    grad_weight = grad_weight.reshape(3, CH, DL).transpose(1, 0, 2)
    grad_taps = sums.reshape(8, 8, CH)[:, :KT].transpose(1, 0, 2).reshape(KT, -1, GROUP).sum(-1)
    return output, grad_tokens, grad_weight, grad_taps


def solution(mesh):
    in_specs = (
        P("col", "depth"),
        P(("row", "col"), None, "depth"),
        P(None, "row"),
        P(("col", "depth"), "row"),
    )
    out_specs = (
        P(("col", "depth"), "row"),
        P("col", "depth"),
        P(("row", "col"), None, "depth"),
        P(None, "row"),
    )
    return jax.shard_map(
        on_device, mesh=mesh, in_specs=in_specs, out_specs=out_specs, check_vma=False
    )
```

```python
import jax
import jax.numpy as jnp
from jax import lax
from jax.experimental import pallas as pl
from jax.experimental.pallas import tpu as pltpu
from jax.sharding import PartitionSpec as P

MESH = pl.DeviceIdType.MESH
F32 = jnp.float32
BF16 = jnp.bfloat16
GROUP = 16
KT = 7
TOK = 768
ROWS = 96
CH = 128
SH = 3 * CH
DL = 1024
HALF = 512
QUARTER = 256


def fma_dot(a, b, dims):
    return lax.dot_general(a, b, (dims, ((), ())), preferred_element_type=F32)


def group_of_channel(channel_axis):
    shape = (2 * HALF // GROUP, 2 * HALF) if channel_axis == 0 else (2 * HALF, 2 * HALF // GROUP)
    groups = lax.broadcasted_iota(jnp.int32, shape, channel_axis)
    channels = lax.broadcasted_iota(jnp.int32, shape, 1 - channel_axis)
    return jnp.where(channels // GROUP == groups, 1.0, 0.0)


def kernel(
    tok_in, w_in, taps_ref, up_in,
    out_ref, gt_ref, gw_ref, ts_ref,
    T, W, SP, U, PP, SB, S, R2, RM, RP, QKV, MX, GF, HM, HG, OB, G,
    TS, TR, TC, TY, TZ, TO, PW, DR, DS, GW, EP, ES, ER, FV,
    l_sem, w_s, w_r, t_s, t_r, u_s, u_r, b_s, b_r, h_s, h_r, c_s, c_r,
    tr_s, tr_r, ty_s, ty_r, tz_s, tz_r, o_s, o_r, d_s, d_r, e_s, e_r, g_s, g_r, f_sem,
):
    r, c, d = lax.axis_index("row"), lax.axis_index("col"), lax.axis_index("depth")
    zl, y, x, k = c // 4, c % 4, d // 2, d % 2
    z = 2 * r + zl

    def znb(delta):
        other = (z + delta + 8) % 8
        return (other // 2, (other % 2) * 4 + y, d)

    def ynb(delta):
        return (r, zl * 4 + (y + delta + 4) % 4, d)

    def xnb(delta):
        return (r, c, ((x + delta + 4) % 4) * 2 + k)

    def dnb(delta):
        return (r, c, (d + delta + 8) % 8)

    sib = (r, c, x * 2 + 1 - k)
    pair = (r, (1 - zl) * 4 + y, d)
    wraps_up = jnp.where(d == 7, 1, 0)
    wraps_down = jnp.where(d == 0, 1, 0)
    following = (r, zl * 4 + (y + wraps_up) % 4, (d + 1) % 8)
    previous = (r, zl * 4 + (y + 4 - wraps_down) % 4, (d + 7) % 8)

    def remote(src, dst, ssem, rsem, to):
        return pltpu.make_async_remote_copy(
            src_ref=src, dst_ref=dst, send_sem=ssem, recv_sem=rsem, device_id=to, device_id_type=MESH
        )

    sends = []

    def send(src, dst, ssem, rsem, to):
        copy = remote(src, dst, ssem, rsem, to)
        copy.start()
        sends.append(copy)

    def arrived(dst, rsem):
        remote(dst, dst, l_sem.at[0], rsem, sib).wait_recv()

    def each(start, stop, step):
        def body(at, carry):
            step(at)
            return carry

        lax.fori_loop(start, stop, body, 0)

    def lanes(at, width):
        return pl.ds(pl.multiple_of(at * width, width), width)

    barrier = pltpu.get_barrier_semaphore()
    partners = [dnb(delta) for delta in range(1, 8)]
    partners += [ynb(delta) for delta in range(1, 4)]
    partners += [znb(delta) for delta in (1, -1, 2, -2)]
    partners += [following, previous]
    for partner in partners:
        pl.semaphore_signal(barrier, inc=1, device_id=partner, device_id_type=MESH)
    locals_ = [
        pltpu.make_async_copy(tok_in, T.at[zl], l_sem.at[1]),
        pltpu.make_async_copy(w_in, W.at[y], l_sem.at[2]),
        pltpu.make_async_copy(up_in.at[:, lanes(zl, HALF)], U.at[zl], l_sem.at[3]),
    ]
    for copy in locals_:
        copy.start()
    pl.semaphore_wait(barrier, len(partners))

    for first, way, side in ((0, 1, 0), (1, -1, 1)):
        for part in (first, 1 - first):
            send(w_in.at[part], W.at[y, part], w_s.at[side, part], w_r.at[side, part], ynb(way))
    send(tok_in.at[pl.ds(0, 384)], T.at[zl, pl.ds(0, 384)], t_s.at[0], t_r.at[0], znb(-1))
    send(tok_in.at[pl.ds(384, 384)], T.at[zl, pl.ds(384, 384)], t_s.at[1], t_r.at[1], znb(1))
    send(up_in.at[:, lanes(1 - zl, HALF)], U.at[zl], u_s.at[0], u_r.at[0], pair)
    for copy in locals_:
        copy.wait()
    spread = lax.dot_general(
        taps_ref[...], group_of_channel(0), (((1,), (0,)), ((), ())), precision=lax.Precision.HIGHEST,
        preferred_element_type=F32,
    )
    for at in range(8):
        SP[at, pl.ds(0, KT)] = spread[:, at * CH : (at + 1) * CH]

    def shard_at(i):
        return (y + (i * (7 - i)) // 2) % 4

    def unit(u):
        return (u + zl) % 2, shard_at(u // 2), 1 - 2 * (u % 2)

    def to_sibling(g, j):
        return remote(PP.at[g, j, :, 1 - k], SB.at[g, j], b_s.at[0, g, j], b_r.at[0, g, j], sib)

    def far(g, j, way):
        return remote(S.at[g, j, (x + 2) % 4], R2.at[g, j], b_s.at[1, g, j], b_r.at[1, g, j], xnb(way))

    def back(g, j, way):
        return remote(
            S.at[g, j, (x - way + 4) % 4], RM.at[g, j], b_s.at[2, g, j], b_r.at[2, g, j], xnb(-way)
        )

    def near(g, j, way):
        return remote(
            S.at[g, j, (x + way + 4) % 4], RP.at[g, j], b_s.at[3, g, j], b_r.at[3, g, j], xnb(way)
        )

    def project(u):
        g, j, _ = unit(u)
        part = fma_dot(T[g], W[j].reshape(SH, DL), ((1,), (1,)))
        PP[g, j] = part.astype(BF16).reshape(4, 2, ROWS, SH)
        to_sibling(g, j).start()

    def chip_sum(u):
        g, j, way = unit(u)
        to_sibling(g, j).wait_recv()
        for at in range(4):
            S[g, j, at] = (PP[g, j, at, k].astype(F32) + SB[g, j, at].astype(F32)).astype(BF16)
        far(g, j, way).start()
        back(g, j, way).start()

    def relay(u):
        g, j, way = unit(u)
        far(g, j, way).wait_recv()
        at = (x + way + 4) % 4
        S[g, j, at] = (S[g, j, at].astype(F32) + R2[g, j].astype(F32)).astype(BF16)
        near(g, j, way).start()

    def relayed_weights(part):
        way = 1 - 2 * part
        rows = W.at[(y - way + 4) % 4, part]
        return remote(rows, rows, w_s.at[2, part], w_r.at[2, part], ynb(way))

    def project_step(u):
        @pl.when(u == 1)
        def _():
            chip_sum(0)
            arrived(W.at[(y + 3) % 4, 0], w_r.at[0, 0])
            relayed_weights(0).start()
            arrived(W.at[(y + 1) % 4, 1], w_r.at[1, 1])
            relayed_weights(1).start()
            relay(0)
            arrived(T.at[1 - zl, pl.ds(0, 384)], t_r.at[0])
            arrived(T.at[1 - zl, pl.ds(384, 384)], t_r.at[1])

        @pl.when(u == 2)
        def _():
            arrived(W.at[(y + 3) % 4, 1], w_r.at[0, 1])

        @pl.when(u == 4)
        def _():
            arrived(W.at[(y + 1) % 4, 0], w_r.at[1, 0])

        @pl.when(u == 6)
        def _():
            chip_sum(5)
            arrived(W.at[(y + 2) % 4, 0], w_r.at[2, 0])
            arrived(W.at[(y + 2) % 4, 1], w_r.at[2, 1])

        project(u)

        @pl.when((u >= 2) & (u != 6))
        def _():
            chip_sum(u - 1)

        @pl.when(u >= 4)
        def _():
            relay(u - 3)

    each(0, 8, project_step)
    chip_sum(7)
    relay(5)

    def mixed_rows(j):
        return remote(MX.at[j, :, pl.ds(ROWS, 8)], HM.at[j], h_s.at[0, j], h_r.at[0, j], following)

    def grad_rows(j):
        return remote(GF.at[j, :, pl.ds(0, 8)], HG.at[j], h_s.at[1, j], h_r.at[1, j], previous)

    def total_step(i):
        for half in range(2):
            g, j, way = unit(2 * i + half)
            back(g, j, way).wait_recv()
            near(g, j, way).wait_recv()
            total = S[g, j, x].astype(F32) + RM[g, j].astype(F32) + RP[g, j].astype(F32)
            total = total.astype(BF16).astype(F32)
            up = U[g, :, lanes(j, CH)].astype(F32)
            QKV[g, j] = total
            MX[j, g, pl.ds(8, ROWS)] = total[:, CH : 2 * CH] * total[:, 2 * CH :]
            GF[j, g, pl.ds(0, ROWS)] = up * total[:, :CH]
        mixed_rows(j).start()
        grad_rows(j).start()

    arrived(U.at[1 - zl], u_r.at[0])
    each(0, 3, total_step)
    each(6, 8, relay)
    each(3, 4, total_step)

    def own_piece(g, j, to_left):
        rows = G.at[g, x, k, :, lanes(j, SH)]
        return remote(rows, rows, c_s.at[to_left, g, j], c_r.at[to_left, g, j], xnb(1 - 2 * to_left))

    def relayed_piece(g, j, to_left):
        way = 1 - 2 * to_left
        rows = G.at[g, (x - way + 4) % 4, k, :, lanes(j, SH)]
        return remote(rows, rows, c_s.at[2, g, j], c_r.at[2, g, j], xnb(way))

    def to_sibling_back(g, j):
        rows = G.at[g, :, k, :, lanes(j, SH)]
        return remote(rows, rows, c_s.at[3, g, j], c_r.at[3, g, j], sib)

    def filter_step(g, i):
        j = shard_at(i)
        if g == 0:
            mixed_rows(j).wait_recv()
            grad_rows(j).wait_recv()
        at_start = (y == 0) & (d == 0)
        at_end = (y == 3) & (d == 7)
        same = jnp.where(at_start, 0.0, 1.0)
        swapped = jnp.where(at_start, 1.0 * g, 0.0)
        MX[j, g, pl.ds(0, 8)] = HM[j, g] * same + HM[j, 1 - g] * swapped
        same = jnp.where(at_end, 0.0, 1.0)
        swapped = jnp.where(at_end, 1.0 - g, 0.0)
        GF[j, g, pl.ds(ROWS, 8)] = HG[j, g] * same + HG[j, 1 - g] * swapped
        taps = SP[zl * 4 + j]
        query = QKV[g, j, :, :CH]
        up = U[g, :, lanes(j, CH)].astype(F32)
        grad = GF[j, g, pl.ds(0, ROWS)]
        filtered = jnp.zeros((ROWS, CH), F32)
        grad_mixed = jnp.zeros((ROWS, CH), F32)
        tap_sums = []
        for o in range(KT):
            shifted = MX[j, g, pl.ds(8 - o, ROWS)]
            tap = taps[o : o + 1]
            filtered = filtered + tap * shifted
            grad_mixed = grad_mixed + tap * GF[j, g, pl.ds(o, ROWS)]
            tap_sums.append(jnp.sum(grad * shifted, axis=0, keepdims=True))
        OB[g, :, lanes(j, CH)] = (query * filtered).astype(BF16)
        G[g, x, k, :, lanes(3 * j, CH)] = (up * filtered).astype(BF16)
        G[g, x, k, :, lanes(3 * j + 1, CH)] = (grad_mixed * QKV[g, j, :, 2 * CH :]).astype(BF16)
        G[g, x, k, :, lanes(3 * j + 2, CH)] = (grad_mixed * QKV[g, j, :, CH : 2 * CH]).astype(BF16)
        TS[g, j] = jnp.concatenate(tap_sums + [jnp.zeros((1, CH), F32)], axis=0)

        own_piece(g, j, 0).start()
        own_piece(g, j, 1).start()

    def relay_piece(g, i):
        j, to_left = shard_at(i), i % 2
        own_piece(g, j, to_left).wait_recv()
        relayed_piece(g, j, to_left).start()

    def sibling_piece(g, i):
        j, to_left = shard_at(i), i % 2
        own_piece(g, j, 1 - to_left).wait_recv()
        relayed_piece(g, j, to_left).wait_recv()
        to_sibling_back(g, j).start()

    def gathered(g, i):
        to_sibling_back(g, shard_at(i)).wait_recv()

    def second_group(i):
        filter_step(1, i)
        sibling_piece(0, i)

    each(0, 4, lambda i: filter_step(0, i))
    each(0, 4, lambda i: relay_piece(0, i))
    each(0, 4, second_group)
    send(OB.at[1 - zl], out_ref.at[:, lanes(zl, HALF)], o_s.at[0], o_r.at[0], pair)
    out_copy = pltpu.make_async_copy(OB.at[zl], out_ref.at[:, lanes(zl, HALF)], l_sem.at[4])
    out_copy.start()
    TC[...] = TS[0] + TS[1]
    for delta in range(1, 8):
        send(TC, TR.at[d], tr_s.at[delta], tr_r.at[d], dnb(delta))
    TR[d] = TC[...]
    each(0, 4, lambda i: gathered(0, i))

    def own_chunk(g, delta, piece):
        return EP[g, piece, lanes(((z + delta + 8) % 8) // 2, 2 * ROWS)]

    def chunk_copy(way, steps, piece):
        return remote(
            ES.at[way, steps, piece], ER.at[way, steps, piece],
            e_s.at[way, steps, piece], e_r.at[way, steps, piece], znb(1 - 2 * way),
        )

    def landed_chunk(way, steps, piece):
        chunk_copy(way, steps, piece).wait_recv()
        return ER[way, steps, piece].astype(F32)

    def send_chunk(g, way, steps, piece, received):
        value = own_chunk(g, steps * (1 - 2 * way), piece)
        if received:
            value = value + landed_chunk(way, steps + 1, piece)
        ES[way, steps, piece] = value.astype(BF16)
        chunk_copy(way, steps, piece).start()

    def token_grads(g, start, stop):
        def step(side):
            both = fma_dot(
                G[g].reshape(TOK, 4 * SH), W[:, :, :, lanes(side, HALF)].reshape(4 * SH, HALF), ((1,), (0,))
            )
            EP[g, 2 * side] = both[:, :QUARTER]
            EP[g, 2 * side + 1] = both[:, QUARTER:]

            @pl.when((zl == g) & (side == 0))
            def _():
                send_chunk(g, 0, 4, 0, False)
                send_chunk(g, 0, 4, 1, False)

            @pl.when((zl == g) & (side == 1))
            def _():
                send_chunk(g, 1, 4, 3, False)
                send_chunk(g, 1, 4, 2, False)

            @pl.when((zl != g) & (side == 0))
            def _():
                send_chunk(g, 1, 3, 1, False)
                send_chunk(g, 1, 3, 0, False)

            @pl.when((zl != g) & (side == 1))
            def _():
                send_chunk(g, 0, 3, 2, False)
                send_chunk(g, 0, 3, 3, False)

        each(start, stop, step)

    def ring_step(g, owner, steps, start, stop):
        @pl.when((zl == g) == owner)
        def _():
            def step(at):
                piece = (at + 2) % 4
                send_chunk(g, 0, steps, piece, True)
                send_chunk(g, 1, steps, 3 - piece, True)

            each(start, stop, step)

    def final_rows(row, piece):
        return gt_ref.at[lanes((row + 4) % 4, 2 * ROWS), lanes(piece, QUARTER)]

    def final_copy(piece, way):
        return remote(
            FV.at[piece], final_rows(r, piece), g_s.at[way, piece], g_r.at[way, piece], znb(2 - 4 * way)
        )

    def final_relay(piece):
        way = piece % 2
        rows = final_rows(r - 1 + 2 * way, piece)
        return remote(rows, rows, g_s.at[2, piece], g_r.at[2, piece], znb(2 - 4 * way))

    def final_own(piece):
        return pltpu.make_async_copy(FV.at[piece], final_rows(r, piece), f_sem.at[piece])

    def finish(g, start, stop):
        @pl.when(zl == g)
        def _():
            def step(at):
                piece = (at + 2) % 4
                total = own_chunk(g, 0, piece) + landed_chunk(0, 1, piece) + landed_chunk(1, 1, piece)
                FV[piece] = total.astype(BF16)
                final_copy(piece, 0).start()
                final_copy(piece, 1).start()
                final_own(piece).start()

            each(start, stop, step)

    def finish_relay(g, start, stop):
        @pl.when(zl == g)
        def _():
            def step(at):
                piece = (at + 2) % 4
                way = piece % 2
                arrived(final_rows(r - 1 + 2 * way, piece), g_r.at[way, piece])
                final_relay(piece).start()

            each(start, stop, step)

    def shard_grad(delta):
        j = (y + delta + 4) % 4
        total = None
        for g in range(2):
            term = fma_dot(G[g, :, :, :, lanes(j, SH)].reshape(TOK, SH), T[g], ((0,), (0,)))
            total = term if total is None else total + term
        return total

    def send_grad(way, kind, value):
        DS[way, kind] = value.astype(BF16)
        send(DS.at[way, kind], DR.at[way, kind], d_s.at[way, kind], d_r.at[way, kind], ynb(1 - 2 * way))

    def landed_grad(way, kind):
        arrived(DR.at[way, kind], d_r.at[way, kind])
        return DR[way, kind].astype(F32)

    cut = SH // 2
    token_grads(0, 0, 2)
    each(0, 4, lambda i: relay_piece(1, i))
    ring_step(0, False, 3, 2, 4)
    ring_step(0, True, 2, 0, 2)
    each(0, 4, lambda i: sibling_piece(1, i))
    each(0, 4, lambda i: gathered(1, i))
    token_grads(1, 0, 1)
    ring_step(0, True, 2, 2, 4)
    token_grads(1, 1, 2)
    ring_step(0, False, 1, 0, 2)
    ring_step(1, False, 3, 2, 4)
    ring_step(0, False, 1, 2, 4)
    part = shard_grad(2)
    send_grad(0, 0, part[:cut])
    send_grad(1, 0, part[cut:])
    ring_step(1, True, 2, 0, 2)
    ring_step(1, True, 2, 2, 4)
    part = shard_grad(1)
    send_grad(0, 1, part[cut:])
    PW[0] = part[:cut]
    ring_step(1, False, 1, 0, 2)
    ring_step(1, False, 1, 2, 4)
    finish(0, 0, 4)
    finish(1, 0, 4)
    part = shard_grad(-1)
    send_grad(1, 1, part[:cut])
    PW[1] = part[cut:]

    for delta in range(1, 8):
        source = (d + delta) % 8
        arrived(TR.at[source], tr_r.at[source])
    total = TR[0]
    for at in range(1, 8):
        total = total + TR[at]
    TZ[...] = total
    TY[y] = total
    for delta in range(1, 4):
        send(TZ, TY.at[y], ty_s.at[delta], ty_r.at[y], ynb(delta))

    send_grad(0, 2, PW[0] + landed_grad(0, 0))
    send_grad(1, 2, PW[1] + landed_grad(1, 0))
    finish_relay(0, 0, 4)
    finish_relay(1, 0, 4)
    GW[...] = shard_grad(0)

    for delta in range(1, 4):
        source = (y + delta) % 4
        arrived(TY.at[source], ty_r.at[source])
    total = TY[0]
    for at in range(1, 4):
        total = total + TY[at]
    TO[zl] = total
    send(TO.at[zl], TO.at[zl], tz_s.at[0], tz_r.at[0], pair)

    GW[pl.ds(0, cut)] = GW[pl.ds(0, cut)] + landed_grad(0, 2) + landed_grad(1, 1)
    GW[pl.ds(cut, cut)] = GW[pl.ds(cut, cut)] + landed_grad(0, 1) + landed_grad(1, 2)
    gw_copy = pltpu.make_async_copy(GW, gw_ref, l_sem.at[5])
    gw_copy.start()

    arrived(TO.at[1 - zl], tz_r.at[0])
    sums = jnp.concatenate([TO[at // 4, at % 4] for at in range(8)], axis=1)
    ts_ref[...] = lax.dot_general(
        sums, group_of_channel(1), (((1,), (0,)), ((), ())), precision=lax.Precision.HIGHEST,
        preferred_element_type=F32,
    )[:KT]
    arrived(out_ref.at[:, lanes(1 - zl, HALF)], o_r.at[0])
    for piece in range(4):
        way = piece % 2
        arrived(final_rows(r + 1 - 2 * way, piece), g_r.at[1 - way, piece])
        arrived(final_rows(r + 2, piece), g_r.at[2, piece])
        final_own(piece).wait()
    out_copy.wait()
    gw_copy.wait()

    for copy in sends:
        copy.wait_send()
    for part in range(2):
        relayed_weights(part).wait_send()

    def sent_piece(piece):
        final_relay(piece).wait_send()
        for way in range(2):
            final_copy(piece, way).wait_send()
            for steps in range(1, 4):
                chunk_copy(way, steps, piece).wait_send()
        chunk_copy(piece // 2, 4, piece).wait_send()

    each(0, 4, sent_piece)

    def sent_step(u):
        g, j, way = unit(u)

        @pl.when(u % 2 == 0)
        def _():
            mixed_rows(j).wait_send()
            grad_rows(j).wait_send()

        for copy in (to_sibling(g, j), far(g, j, way), back(g, j, way), near(g, j, way)):
            copy.wait_send()
        for copy in (
            own_piece(g, j, 0), own_piece(g, j, 1), relayed_piece(g, j, (u // 2) % 2), to_sibling_back(g, j)
        ):
            copy.wait_send()

    each(0, 8, sent_step)


def hand_over(out_in, gt_in, gw_in, taps_in, out_ref, gt_ref, gw_ref, taps_ref, out_v, gt_v, gw_v, sem):
    steps = []
    for src, held, dst, parts in ((gt_in, gt_v, gt_ref, 4), (gw_in, gw_v, gw_ref, 4), (out_in, out_v, out_ref, 1)):
        rows = held.shape[0] // parts
        for part in range(parts):
            at = pl.ds(part * rows, rows)
            steps.append((src.at[at], held.at[at], dst.at[at]))
    reads = [pltpu.make_async_copy(src, held, sem.at[0, n]) for n, (src, held, _) in enumerate(steps)]
    writes = [pltpu.make_async_copy(held, dst, sem.at[1, n]) for n, (_, held, dst) in enumerate(steps)]
    for copy in reads:
        copy.start()
    taps_ref[...] = taps_in[...]
    for read, write in zip(reads, writes):
        read.wait()
        write.start()
    for copy in writes:
        copy.wait()


def on_device(tokens, weight, taps, upstream):
    shard = weight.transpose(1, 0, 2).reshape(2, SH // 2, DL)
    vmem = pl.BlockSpec(memory_space=pltpu.VMEM)
    anywhere = pl.BlockSpec(memory_space=pl.ANY)
    dma = pltpu.SemaphoreType.DMA
    scratch = [
        pltpu.VMEM((2, TOK, DL), BF16),
        pltpu.VMEM((4, 2, SH // 2, DL), BF16),
        pltpu.VMEM((8, 8, CH), F32),
        pltpu.VMEM((2, ROWS, HALF), BF16),
        pltpu.VMEM((2, 4, 4, 2, ROWS, SH), BF16),
        pltpu.VMEM((2, 4, 4, ROWS, SH), BF16),
        pltpu.VMEM((2, 4, 4, ROWS, SH), BF16),
        pltpu.VMEM((2, 4, ROWS, SH), BF16),
        pltpu.VMEM((2, 4, ROWS, SH), BF16),
        pltpu.VMEM((2, 4, ROWS, SH), BF16),
        pltpu.VMEM((2, 4, ROWS, SH), F32),
        pltpu.VMEM((4, 2, ROWS + 8, CH), F32),
        pltpu.VMEM((4, 2, ROWS + 8, CH), F32),
        pltpu.VMEM((4, 2, 8, CH), F32),
        pltpu.VMEM((4, 2, 8, CH), F32),
        pltpu.VMEM((2, ROWS, HALF), BF16),
        pltpu.VMEM((2, 4, 2, ROWS, 4 * SH), BF16),
        pltpu.VMEM((2, 4, 8, CH), F32),
        pltpu.VMEM((8, 4, 8, CH), F32),
        pltpu.VMEM((4, 8, CH), F32),
        pltpu.VMEM((4, 4, 8, CH), F32),
        pltpu.VMEM((4, 8, CH), F32),
        pltpu.VMEM((2, 4, 8, CH), F32),
        pltpu.VMEM((2, SH // 2, DL), F32),
        pltpu.VMEM((2, 3, SH // 2, DL), BF16),
        pltpu.VMEM((2, 3, SH // 2, DL), BF16),
        pltpu.VMEM((SH, DL), F32),
        pltpu.VMEM((2, 4, TOK, QUARTER), F32),
        pltpu.VMEM((2, 5, 4, 2 * ROWS, QUARTER), BF16),
        pltpu.VMEM((2, 5, 4, 2 * ROWS, QUARTER), BF16),
        pltpu.VMEM((4, 2 * ROWS, QUARTER), BF16),
        dma((6,)),
        dma((3, 2)), dma((3, 2)),
        dma((2,)), dma((2,)),
        dma((1,)), dma((1,)),
        dma((4, 2, 4)), dma((4, 2, 4)),
        dma((2, 4)), dma((2, 4)),
        dma((4, 2, 4)), dma((4, 2, 4)),
        dma((8,)), dma((8,)),
        dma((4,)), dma((4,)),
        dma((1,)), dma((1,)),
        dma((1,)), dma((1,)),
        dma((2, 3)), dma((2, 3)),
        dma((2, 5, 4)), dma((2, 5, 4)),
        dma((3, 4)), dma((3, 4)),
        dma((4,)),
    ]
    shapes = (
        jax.ShapeDtypeStruct((ROWS, 2 * HALF), BF16),
        jax.ShapeDtypeStruct((TOK, DL), BF16),
        jax.ShapeDtypeStruct((SH, DL), F32),
        jax.ShapeDtypeStruct((KT, 2 * HALF // GROUP), F32),
    )
    results = pl.pallas_call(
        kernel,
        out_shape=tuple(pltpu.VMEM(shape.shape, shape.dtype) for shape in shapes),
        in_specs=[anywhere, anywhere, vmem, anywhere],
        out_specs=(vmem, vmem, vmem, vmem),
        scratch_shapes=scratch,
        compiler_params=pltpu.CompilerParams(
            collective_id=0, has_side_effects=True, vmem_limit_bytes=58 * 1024 * 1024
        ),
        cost_estimate=pl.CostEstimate(
            flops=6 * TOK * DL * 8 * SH, bytes_accessed=8 * 1024 * 1024, transcendentals=0
        ),
    )(tokens, shard, taps, upstream)
    output, grad_tokens, grad_weight, grad_taps = results
    grad_weight = grad_weight.reshape(3, CH, DL).transpose(1, 0, 2)
    return output, grad_tokens, grad_weight, grad_taps


def solution(mesh):
    in_specs = (
        P("col", "depth"),
        P(("row", "col"), None, "depth"),
        P(None, "row"),
        P(("col", "depth"), "row"),
    )
    out_specs = (
        P(("col", "depth"), "row"),
        P("col", "depth"),
        P(("row", "col"), None, "depth"),
        P(None, "row"),
    )
    return jax.shard_map(
        on_device, mesh=mesh, in_specs=in_specs, out_specs=out_specs, check_vma=False
    )
```

```python
import jax
import jax.numpy as jnp
from jax import lax
from jax.experimental import pallas as pl
from jax.experimental.pallas import tpu as pltpu
from jax.sharding import PartitionSpec as P

MESH = pl.DeviceIdType.MESH
F32 = jnp.float32
BF16 = jnp.bfloat16
GROUP = 16
KT = 7
TOK = 768
ROWS = 96
CH = 128
SH = 3 * CH
DL = 1024
HALF = 512
QUARTER = 256


def fma_dot(a, b, dims):
    return lax.dot_general(a, b, (dims, ((), ())), preferred_element_type=F32)


def group_of_channel(channel_axis):
    shape = (2 * HALF // GROUP, 2 * HALF) if channel_axis == 0 else (2 * HALF, 2 * HALF // GROUP)
    groups = lax.broadcasted_iota(jnp.int32, shape, channel_axis)
    channels = lax.broadcasted_iota(jnp.int32, shape, 1 - channel_axis)
    return jnp.where(channels // GROUP == groups, 1.0, 0.0)


def kernel(
    tok_in, w_in, taps_ref, up_in,
    out_ref, gt_ref, gw_ref, ts_ref,
    T, W, SP, U, PP, SB, S, R2, RM, RP, QKV, MX, GF, HM, HG, OB, G,
    TS, TR, TC, TY, TZ, TO, PW, DR, DS, GW, EP, ES, ER, FV,
    l_sem, w_s, w_r, t_s, t_r, u_s, u_r, b_s, b_r, h_s, h_r, c_s, c_r,
    tr_s, tr_r, ty_s, ty_r, tz_s, tz_r, o_s, o_r, d_s, d_r, e_s, e_r, g_s, g_r, f_sem,
):
    r, c, d = lax.axis_index("row"), lax.axis_index("col"), lax.axis_index("depth")
    zl, y, x, k = c // 4, c % 4, d // 2, d % 2
    z = 2 * r + zl

    def znb(delta):
        other = (z + delta + 8) % 8
        return (other // 2, (other % 2) * 4 + y, d)

    def ynb(delta):
        return (r, zl * 4 + (y + delta + 4) % 4, d)

    def xnb(delta):
        return (r, c, ((x + delta + 4) % 4) * 2 + k)

    def dnb(delta):
        return (r, c, (d + delta + 8) % 8)

    sib = (r, c, x * 2 + 1 - k)
    pair = (r, (1 - zl) * 4 + y, d)
    wraps_up = jnp.where(d == 7, 1, 0)
    wraps_down = jnp.where(d == 0, 1, 0)
    following = (r, zl * 4 + (y + wraps_up) % 4, (d + 1) % 8)
    previous = (r, zl * 4 + (y + 4 - wraps_down) % 4, (d + 7) % 8)

    def remote(src, dst, ssem, rsem, to):
        return pltpu.make_async_remote_copy(
            src_ref=src, dst_ref=dst, send_sem=ssem, recv_sem=rsem, device_id=to, device_id_type=MESH
        )

    sends = []

    def send(src, dst, ssem, rsem, to):
        copy = remote(src, dst, ssem, rsem, to)
        copy.start()
        sends.append(copy)

    def arrived(dst, rsem):
        remote(dst, dst, l_sem.at[0], rsem, sib).wait_recv()

    def each(start, stop, step):
        def body(at, carry):
            step(at)
            return carry

        lax.fori_loop(start, stop, body, 0)

    def lanes(at, width):
        return pl.ds(pl.multiple_of(at * width, width), width)

    barrier = pltpu.get_barrier_semaphore()
    partners = [dnb(delta) for delta in range(1, 8)]
    partners += [ynb(delta) for delta in range(1, 4)]
    partners += [znb(delta) for delta in (1, -1, 2, -2)]
    partners += [following, previous]
    for partner in partners:
        pl.semaphore_signal(barrier, inc=1, device_id=partner, device_id_type=MESH)
    locals_ = [
        pltpu.make_async_copy(tok_in, T.at[zl], l_sem.at[1]),
        pltpu.make_async_copy(w_in, W.at[y], l_sem.at[2]),
        pltpu.make_async_copy(up_in.at[:, lanes(zl, HALF)], U.at[zl], l_sem.at[3]),
    ]
    for copy in locals_:
        copy.start()
    pl.semaphore_wait(barrier, len(partners))

    for first, way, side in ((0, 1, 0), (1, -1, 1)):
        for part in (first, 1 - first):
            send(w_in.at[part], W.at[y, part], w_s.at[side, part], w_r.at[side, part], ynb(way))
    send(tok_in.at[pl.ds(0, 384)], T.at[zl, pl.ds(0, 384)], t_s.at[0], t_r.at[0], znb(-1))
    send(tok_in.at[pl.ds(384, 384)], T.at[zl, pl.ds(384, 384)], t_s.at[1], t_r.at[1], znb(1))
    send(up_in.at[:, lanes(1 - zl, HALF)], U.at[zl], u_s.at[0], u_r.at[0], pair)
    for copy in locals_:
        copy.wait()
    spread = lax.dot_general(
        taps_ref[...], group_of_channel(0), (((1,), (0,)), ((), ())), precision=lax.Precision.HIGHEST,
        preferred_element_type=F32,
    )
    for at in range(8):
        SP[at, pl.ds(0, KT)] = spread[:, at * CH : (at + 1) * CH]

    def shard_at(i):
        return (y + (i * (7 - i)) // 2) % 4

    def unit(u):
        return (u + zl) % 2, shard_at(u // 2), 1 - 2 * (u % 2)

    def to_sibling(g, j):
        return remote(PP.at[g, j, :, 1 - k], SB.at[g, j], b_s.at[0, g, j], b_r.at[0, g, j], sib)

    def far(g, j, way):
        return remote(S.at[g, j, (x + 2) % 4], R2.at[g, j], b_s.at[1, g, j], b_r.at[1, g, j], xnb(way))

    def back(g, j, way):
        return remote(
            S.at[g, j, (x - way + 4) % 4], RM.at[g, j], b_s.at[2, g, j], b_r.at[2, g, j], xnb(-way)
        )

    def near(g, j, way):
        return remote(
            S.at[g, j, (x + way + 4) % 4], RP.at[g, j], b_s.at[3, g, j], b_r.at[3, g, j], xnb(way)
        )

    def project(u):
        g, j, _ = unit(u)
        part = fma_dot(T[g], W[j].reshape(SH, DL), ((1,), (1,)))
        PP[g, j] = part.astype(BF16).reshape(4, 2, ROWS, SH)
        to_sibling(g, j).start()

    def chip_sum(u):
        g, j, way = unit(u)
        to_sibling(g, j).wait_recv()
        for at in range(4):
            S[g, j, at] = (PP[g, j, at, k].astype(F32) + SB[g, j, at].astype(F32)).astype(BF16)
        far(g, j, way).start()
        back(g, j, way).start()

    def relay(u):
        g, j, way = unit(u)
        far(g, j, way).wait_recv()
        at = (x + way + 4) % 4
        S[g, j, at] = (S[g, j, at].astype(F32) + R2[g, j].astype(F32)).astype(BF16)
        near(g, j, way).start()

    def relayed_weights(part):
        way = 1 - 2 * part
        rows = W.at[(y - way + 4) % 4, part]
        return remote(rows, rows, w_s.at[2, part], w_r.at[2, part], ynb(way))

    def project_step(u):
        @pl.when(u == 1)
        def _():
            chip_sum(0)
            arrived(W.at[(y + 3) % 4, 0], w_r.at[0, 0])
            relayed_weights(0).start()
            arrived(W.at[(y + 1) % 4, 1], w_r.at[1, 1])
            relayed_weights(1).start()
            relay(0)
            arrived(T.at[1 - zl, pl.ds(0, 384)], t_r.at[0])
            arrived(T.at[1 - zl, pl.ds(384, 384)], t_r.at[1])

        @pl.when(u == 2)
        def _():
            arrived(W.at[(y + 3) % 4, 1], w_r.at[0, 1])

        @pl.when(u == 4)
        def _():
            arrived(W.at[(y + 1) % 4, 0], w_r.at[1, 0])

        @pl.when(u == 6)
        def _():
            chip_sum(5)
            arrived(W.at[(y + 2) % 4, 0], w_r.at[2, 0])
            arrived(W.at[(y + 2) % 4, 1], w_r.at[2, 1])

        project(u)

        @pl.when((u >= 2) & (u != 6))
        def _():
            chip_sum(u - 1)

        @pl.when(u >= 4)
        def _():
            relay(u - 3)

    each(0, 8, project_step)
    chip_sum(7)
    relay(5)

    def mixed_rows(j):
        return remote(MX.at[j, :, pl.ds(ROWS, 8)], HM.at[j], h_s.at[0, j], h_r.at[0, j], following)

    def grad_rows(j):
        return remote(GF.at[j, :, pl.ds(0, 8)], HG.at[j], h_s.at[1, j], h_r.at[1, j], previous)

    def total_step(i):
        for half in range(2):
            g, j, way = unit(2 * i + half)
            back(g, j, way).wait_recv()
            near(g, j, way).wait_recv()
            total = S[g, j, x].astype(F32) + RM[g, j].astype(F32) + RP[g, j].astype(F32)
            total = total.astype(BF16).astype(F32)
            up = U[g, :, lanes(j, CH)].astype(F32)
            QKV[g, j] = total
            MX[j, g, pl.ds(8, ROWS)] = total[:, CH : 2 * CH] * total[:, 2 * CH :]
            GF[j, g, pl.ds(0, ROWS)] = up * total[:, :CH]
        mixed_rows(j).start()
        grad_rows(j).start()

    arrived(U.at[1 - zl], u_r.at[0])
    each(0, 3, total_step)
    each(6, 8, relay)
    each(3, 4, total_step)

    def own_piece(g, j, to_left):
        rows = G.at[g, x, k, :, lanes(j, SH)]
        return remote(rows, rows, c_s.at[to_left, g, j], c_r.at[to_left, g, j], xnb(1 - 2 * to_left))

    def relayed_piece(g, j, to_left):
        way = 1 - 2 * to_left
        rows = G.at[g, (x - way + 4) % 4, k, :, lanes(j, SH)]
        return remote(rows, rows, c_s.at[2, g, j], c_r.at[2, g, j], xnb(way))

    def to_sibling_back(g, j):
        rows = G.at[g, :, k, :, lanes(j, SH)]
        return remote(rows, rows, c_s.at[3, g, j], c_r.at[3, g, j], sib)

    def filter_step(g, i):
        j = shard_at(i)
        if g == 0:
            mixed_rows(j).wait_recv()
            grad_rows(j).wait_recv()
        at_start = (y == 0) & (d == 0)
        at_end = (y == 3) & (d == 7)
        same = jnp.where(at_start, 0.0, 1.0)
        swapped = jnp.where(at_start, 1.0 * g, 0.0)
        MX[j, g, pl.ds(0, 8)] = HM[j, g] * same + HM[j, 1 - g] * swapped
        same = jnp.where(at_end, 0.0, 1.0)
        swapped = jnp.where(at_end, 1.0 - g, 0.0)
        GF[j, g, pl.ds(ROWS, 8)] = HG[j, g] * same + HG[j, 1 - g] * swapped
        taps = SP[zl * 4 + j]
        query = QKV[g, j, :, :CH]
        up = U[g, :, lanes(j, CH)].astype(F32)
        grad = GF[j, g, pl.ds(0, ROWS)]
        filtered = jnp.zeros((ROWS, CH), F32)
        grad_mixed = jnp.zeros((ROWS, CH), F32)
        tap_sums = []
        for o in range(KT):
            shifted = MX[j, g, pl.ds(8 - o, ROWS)]
            tap = taps[o : o + 1]
            filtered = filtered + tap * shifted
            grad_mixed = grad_mixed + tap * GF[j, g, pl.ds(o, ROWS)]
            tap_sums.append(jnp.sum(grad * shifted, axis=0, keepdims=True))
        OB[g, :, lanes(j, CH)] = (query * filtered).astype(BF16)
        G[g, x, k, :, lanes(3 * j, CH)] = (up * filtered).astype(BF16)
        G[g, x, k, :, lanes(3 * j + 1, CH)] = (grad_mixed * QKV[g, j, :, 2 * CH :]).astype(BF16)
        G[g, x, k, :, lanes(3 * j + 2, CH)] = (grad_mixed * QKV[g, j, :, CH : 2 * CH]).astype(BF16)
        TS[g, j] = jnp.concatenate(tap_sums + [jnp.zeros((1, CH), F32)], axis=0)

        own_piece(g, j, 0).start()
        own_piece(g, j, 1).start()

    def relay_piece(g, i):
        j, to_left = shard_at(i), i % 2
        own_piece(g, j, to_left).wait_recv()
        relayed_piece(g, j, to_left).start()

    def sibling_piece(g, i):
        j, to_left = shard_at(i), i % 2
        own_piece(g, j, 1 - to_left).wait_recv()
        relayed_piece(g, j, to_left).wait_recv()
        to_sibling_back(g, j).start()

    def gathered(g, i):
        to_sibling_back(g, shard_at(i)).wait_recv()

    def second_group(i):
        filter_step(1, i)
        sibling_piece(0, i)

    each(0, 4, lambda i: filter_step(0, i))
    each(0, 4, lambda i: relay_piece(0, i))
    each(0, 4, second_group)
    send(OB.at[1 - zl], out_ref.at[:, lanes(zl, HALF)], o_s.at[0], o_r.at[0], pair)
    out_copy = pltpu.make_async_copy(OB.at[zl], out_ref.at[:, lanes(zl, HALF)], l_sem.at[4])
    out_copy.start()
    TC[...] = TS[0] + TS[1]
    for delta in range(1, 8):
        send(TC, TR.at[d], tr_s.at[delta], tr_r.at[d], dnb(delta))
    TR[d] = TC[...]

    def own_chunk(g, delta, piece):
        return EP[g, piece, lanes(((z + delta + 8) % 8) // 2, 2 * ROWS)]

    def chunk_copy(way, steps, piece):
        return remote(
            ES.at[way, steps, piece], ER.at[way, steps, piece],
            e_s.at[way, steps, piece], e_r.at[way, steps, piece], znb(1 - 2 * way),
        )

    def landed_chunk(way, steps, piece):
        chunk_copy(way, steps, piece).wait_recv()
        return ER[way, steps, piece].astype(F32)

    def send_chunk(g, way, steps, piece, received):
        value = own_chunk(g, steps * (1 - 2 * way), piece)
        if received:
            value = value + landed_chunk(way, steps + 1, piece)
        ES[way, steps, piece] = value.astype(BF16)
        chunk_copy(way, steps, piece).start()

    def shard_product(g, i, side):
        j = shard_at(i)
        rows = G[g, :, :, :, lanes(j, SH)].reshape(TOK, SH)
        return fma_dot(rows, W[j, :, :, lanes(side, HALF)].reshape(SH, HALF), ((1,), (0,)))

    def add_shard(g, i):
        gathered(g, i)
        for side in range(2):
            both = shard_product(g, i, side)
            for half in range(2):
                term = both[:, half * QUARTER : (half + 1) * QUARTER]
                if isinstance(i, int):
                    EP[g, 2 * side + half] = term
                else:
                    EP[g, 2 * side + half] += term

    def add_last_shard(g):
        gathered(g, 3)

        def step(side):
            both = shard_product(g, 3, side)
            EP[g, 2 * side] += both[:, :QUARTER]
            EP[g, 2 * side + 1] += both[:, QUARTER:]

            @pl.when((zl == g) & (side == 0))
            def _():
                send_chunk(g, 0, 4, 0, False)
                send_chunk(g, 0, 4, 1, False)

            @pl.when((zl == g) & (side == 1))
            def _():
                send_chunk(g, 1, 4, 3, False)
                send_chunk(g, 1, 4, 2, False)

            @pl.when((zl != g) & (side == 0))
            def _():
                send_chunk(g, 1, 3, 1, False)
                send_chunk(g, 1, 3, 0, False)

            @pl.when((zl != g) & (side == 1))
            def _():
                send_chunk(g, 0, 3, 2, False)
                send_chunk(g, 0, 3, 3, False)

        each(0, 2, step)

    def ring_step(g, owner, steps, start, stop):
        @pl.when((zl == g) == owner)
        def _():
            def step(at):
                piece = (at + 2) % 4
                send_chunk(g, 0, steps, piece, True)
                send_chunk(g, 1, steps, 3 - piece, True)

            each(start, stop, step)

    def final_rows(row, piece):
        return gt_ref.at[lanes((row + 4) % 4, 2 * ROWS), lanes(piece, QUARTER)]

    def final_copy(piece, way):
        return remote(
            FV.at[piece], final_rows(r, piece), g_s.at[way, piece], g_r.at[way, piece], znb(2 - 4 * way)
        )

    def final_relay(piece):
        way = piece % 2
        rows = final_rows(r - 1 + 2 * way, piece)
        return remote(rows, rows, g_s.at[2, piece], g_r.at[2, piece], znb(2 - 4 * way))

    def final_own(piece):
        return pltpu.make_async_copy(FV.at[piece], final_rows(r, piece), f_sem.at[piece])

    def finish(g, start, stop):
        @pl.when(zl == g)
        def _():
            def step(at):
                piece = (at + 2) % 4
                total = own_chunk(g, 0, piece) + landed_chunk(0, 1, piece) + landed_chunk(1, 1, piece)
                FV[piece] = total.astype(BF16)
                final_copy(piece, 0).start()
                final_copy(piece, 1).start()
                final_own(piece).start()

            each(start, stop, step)

    def finish_relay(g, start, stop):
        @pl.when(zl == g)
        def _():
            def step(at):
                piece = (at + 2) % 4
                way = piece % 2
                arrived(final_rows(r - 1 + 2 * way, piece), g_r.at[way, piece])
                final_relay(piece).start()

            each(start, stop, step)

    def shard_grad(delta):
        j = (y + delta + 4) % 4
        total = None
        for g in range(2):
            term = fma_dot(G[g, :, :, :, lanes(j, SH)].reshape(TOK, SH), T[g], ((0,), (0,)))
            total = term if total is None else total + term
        return total

    def send_grad(way, kind, value):
        DS[way, kind] = value.astype(BF16)
        send(DS.at[way, kind], DR.at[way, kind], d_s.at[way, kind], d_r.at[way, kind], ynb(1 - 2 * way))

    def landed_grad(way, kind):
        arrived(DR.at[way, kind], d_r.at[way, kind])
        return DR[way, kind].astype(F32)

    cut = SH // 2
    add_shard(0, 0)
    each(1, 3, lambda i: add_shard(0, i))
    each(0, 2, lambda i: relay_piece(1, i))
    add_last_shard(0)
    each(2, 4, lambda i: relay_piece(1, i))
    ring_step(0, False, 3, 2, 4)
    ring_step(0, True, 2, 0, 2)
    each(0, 4, lambda i: sibling_piece(1, i))
    add_shard(1, 0)
    ring_step(0, True, 2, 2, 4)
    each(1, 3, lambda i: add_shard(1, i))
    ring_step(0, False, 1, 0, 2)
    add_last_shard(1)
    ring_step(1, False, 3, 2, 4)
    ring_step(0, False, 1, 2, 4)
    part = shard_grad(2)
    send_grad(0, 0, part[:cut])
    send_grad(1, 0, part[cut:])
    ring_step(1, True, 2, 0, 2)
    ring_step(1, True, 2, 2, 4)
    ring_step(1, False, 1, 0, 2)
    ring_step(1, False, 1, 2, 4)
    finish(0, 0, 4)
    finish(1, 0, 4)
    part = shard_grad(1)
    send_grad(0, 1, part[cut:])
    PW[0] = part[:cut]
    part = shard_grad(-1)
    send_grad(1, 1, part[:cut])
    PW[1] = part[cut:]

    for delta in range(1, 8):
        source = (d + delta) % 8
        arrived(TR.at[source], tr_r.at[source])
    total = TR[0]
    for at in range(1, 8):
        total = total + TR[at]
    TZ[...] = total
    TY[y] = total
    for delta in range(1, 4):
        send(TZ, TY.at[y], ty_s.at[delta], ty_r.at[y], ynb(delta))

    send_grad(0, 2, PW[0] + landed_grad(0, 0))
    send_grad(1, 2, PW[1] + landed_grad(1, 0))
    finish_relay(0, 0, 4)
    finish_relay(1, 0, 4)
    GW[...] = shard_grad(0)

    for delta in range(1, 4):
        source = (y + delta) % 4
        arrived(TY.at[source], ty_r.at[source])
    total = TY[0]
    for at in range(1, 4):
        total = total + TY[at]
    TO[zl] = total
    send(TO.at[zl], TO.at[zl], tz_s.at[0], tz_r.at[0], pair)

    GW[pl.ds(0, cut)] = GW[pl.ds(0, cut)] + landed_grad(0, 2) + landed_grad(1, 1)
    GW[pl.ds(cut, cut)] = GW[pl.ds(cut, cut)] + landed_grad(0, 1) + landed_grad(1, 2)
    gw_copy = pltpu.make_async_copy(GW, gw_ref, l_sem.at[5])
    gw_copy.start()

    arrived(TO.at[1 - zl], tz_r.at[0])
    sums = jnp.concatenate([TO[at // 4, at % 4] for at in range(8)], axis=1)
    ts_ref[...] = lax.dot_general(
        sums, group_of_channel(1), (((1,), (0,)), ((), ())), precision=lax.Precision.HIGHEST,
        preferred_element_type=F32,
    )[:KT]
    arrived(out_ref.at[:, lanes(1 - zl, HALF)], o_r.at[0])
    for piece in range(4):
        way = piece % 2
        arrived(final_rows(r + 1 - 2 * way, piece), g_r.at[1 - way, piece])
        arrived(final_rows(r + 2, piece), g_r.at[2, piece])
        final_own(piece).wait()
    out_copy.wait()
    gw_copy.wait()

    for copy in sends:
        copy.wait_send()
    for part in range(2):
        relayed_weights(part).wait_send()

    def sent_piece(piece):
        final_relay(piece).wait_send()
        for way in range(2):
            final_copy(piece, way).wait_send()
            for steps in range(1, 4):
                chunk_copy(way, steps, piece).wait_send()
        chunk_copy(piece // 2, 4, piece).wait_send()

    each(0, 4, sent_piece)

    def sent_step(u):
        g, j, way = unit(u)

        @pl.when(u % 2 == 0)
        def _():
            mixed_rows(j).wait_send()
            grad_rows(j).wait_send()

        for copy in (to_sibling(g, j), far(g, j, way), back(g, j, way), near(g, j, way)):
            copy.wait_send()
        for copy in (
            own_piece(g, j, 0), own_piece(g, j, 1), relayed_piece(g, j, (u // 2) % 2), to_sibling_back(g, j)
        ):
            copy.wait_send()

    each(0, 8, sent_step)


def hand_over(out_in, gt_in, gw_in, taps_in, out_ref, gt_ref, gw_ref, taps_ref, out_v, gt_v, gw_v, sem):
    steps = []
    for src, held, dst, parts in ((gt_in, gt_v, gt_ref, 4), (gw_in, gw_v, gw_ref, 4), (out_in, out_v, out_ref, 1)):
        rows = held.shape[0] // parts
        for part in range(parts):
            at = pl.ds(part * rows, rows)
            steps.append((src.at[at], held.at[at], dst.at[at]))
    reads = [pltpu.make_async_copy(src, held, sem.at[0, n]) for n, (src, held, _) in enumerate(steps)]
    writes = [pltpu.make_async_copy(held, dst, sem.at[1, n]) for n, (_, held, dst) in enumerate(steps)]
    for copy in reads:
        copy.start()
    taps_ref[...] = taps_in[...]
    for read, write in zip(reads, writes):
        read.wait()
        write.start()
    for copy in writes:
        copy.wait()


def on_device(tokens, weight, taps, upstream):
    shard = weight.transpose(1, 0, 2).reshape(2, SH // 2, DL)
    vmem = pl.BlockSpec(memory_space=pltpu.VMEM)
    anywhere = pl.BlockSpec(memory_space=pl.ANY)
    dma = pltpu.SemaphoreType.DMA
    scratch = [
        pltpu.VMEM((2, TOK, DL), BF16),
        pltpu.VMEM((4, 2, SH // 2, DL), BF16),
        pltpu.VMEM((8, 8, CH), F32),
        pltpu.VMEM((2, ROWS, HALF), BF16),
        pltpu.VMEM((2, 4, 4, 2, ROWS, SH), BF16),
        pltpu.VMEM((2, 4, 4, ROWS, SH), BF16),
        pltpu.VMEM((2, 4, 4, ROWS, SH), BF16),
        pltpu.VMEM((2, 4, ROWS, SH), BF16),
        pltpu.VMEM((2, 4, ROWS, SH), BF16),
        pltpu.VMEM((2, 4, ROWS, SH), BF16),
        pltpu.VMEM((2, 4, ROWS, SH), F32),
        pltpu.VMEM((4, 2, ROWS + 8, CH), F32),
        pltpu.VMEM((4, 2, ROWS + 8, CH), F32),
        pltpu.VMEM((4, 2, 8, CH), F32),
        pltpu.VMEM((4, 2, 8, CH), F32),
        pltpu.VMEM((2, ROWS, HALF), BF16),
        pltpu.VMEM((2, 4, 2, ROWS, 4 * SH), BF16),
        pltpu.VMEM((2, 4, 8, CH), F32),
        pltpu.VMEM((8, 4, 8, CH), F32),
        pltpu.VMEM((4, 8, CH), F32),
        pltpu.VMEM((4, 4, 8, CH), F32),
        pltpu.VMEM((4, 8, CH), F32),
        pltpu.VMEM((2, 4, 8, CH), F32),
        pltpu.VMEM((2, SH // 2, DL), F32),
        pltpu.VMEM((2, 3, SH // 2, DL), BF16),
        pltpu.VMEM((2, 3, SH // 2, DL), BF16),
        pltpu.VMEM((SH, DL), F32),
        pltpu.VMEM((2, 4, TOK, QUARTER), F32),
        pltpu.VMEM((2, 5, 4, 2 * ROWS, QUARTER), BF16),
        pltpu.VMEM((2, 5, 4, 2 * ROWS, QUARTER), BF16),
        pltpu.VMEM((4, 2 * ROWS, QUARTER), BF16),
        dma((6,)),
        dma((3, 2)), dma((3, 2)),
        dma((2,)), dma((2,)),
        dma((1,)), dma((1,)),
        dma((4, 2, 4)), dma((4, 2, 4)),
        dma((2, 4)), dma((2, 4)),
        dma((4, 2, 4)), dma((4, 2, 4)),
        dma((8,)), dma((8,)),
        dma((4,)), dma((4,)),
        dma((1,)), dma((1,)),
        dma((1,)), dma((1,)),
        dma((2, 3)), dma((2, 3)),
        dma((2, 5, 4)), dma((2, 5, 4)),
        dma((3, 4)), dma((3, 4)),
        dma((4,)),
    ]
    shapes = (
        jax.ShapeDtypeStruct((ROWS, 2 * HALF), BF16),
        jax.ShapeDtypeStruct((TOK, DL), BF16),
        jax.ShapeDtypeStruct((SH, DL), F32),
        jax.ShapeDtypeStruct((KT, 2 * HALF // GROUP), F32),
    )
    results = pl.pallas_call(
        kernel,
        out_shape=tuple(pltpu.VMEM(shape.shape, shape.dtype) for shape in shapes),
        in_specs=[anywhere, anywhere, vmem, anywhere],
        out_specs=(vmem, vmem, vmem, vmem),
        scratch_shapes=scratch,
        compiler_params=pltpu.CompilerParams(
            collective_id=0, has_side_effects=True, vmem_limit_bytes=58 * 1024 * 1024
        ),
        cost_estimate=pl.CostEstimate(
            flops=6 * TOK * DL * 8 * SH, bytes_accessed=8 * 1024 * 1024, transcendentals=0
        ),
    )(tokens, shard, taps, upstream)
    output, grad_tokens, grad_weight, grad_taps = results
    grad_weight = grad_weight.reshape(3, CH, DL).transpose(1, 0, 2)
    return output, grad_tokens, grad_weight, grad_taps


def solution(mesh):
    in_specs = (
        P("col", "depth"),
        P(("row", "col"), None, "depth"),
        P(None, "row"),
        P(("col", "depth"), "row"),
    )
    out_specs = (
        P(("col", "depth"), "row"),
        P("col", "depth"),
        P(("row", "col"), None, "depth"),
        P(None, "row"),
    )
    return jax.shard_map(
        on_device, mesh=mesh, in_specs=in_specs, out_specs=out_specs, check_vma=False
    )
```

```python
import jax
import jax.numpy as jnp
from jax import lax
from jax.experimental import pallas as pl
from jax.experimental.pallas import tpu as pltpu
from jax.sharding import PartitionSpec as P

MESH = pl.DeviceIdType.MESH
F32 = jnp.float32
BF16 = jnp.bfloat16
GROUP = 16
KT = 7
TOK = 768
ROWS = 96
CH = 128
SH = 3 * CH
DL = 1024
HALF = 512
QUARTER = 256


def fma_dot(a, b, dims):
    return lax.dot_general(a, b, (dims, ((), ())), preferred_element_type=F32)


def group_of_channel(channel_axis):
    shape = (2 * HALF // GROUP, 2 * HALF) if channel_axis == 0 else (2 * HALF, 2 * HALF // GROUP)
    groups = lax.broadcasted_iota(jnp.int32, shape, channel_axis)
    channels = lax.broadcasted_iota(jnp.int32, shape, 1 - channel_axis)
    return jnp.where(channels // GROUP == groups, 1.0, 0.0)


def kernel(
    tok_in, w_in, taps_ref, up_in,
    out_ref, gt_ref, gw_ref, ts_ref,
    T, W, SP, U, PP, SB, S, R2, RM, RP, QKV, MX, GF, HM, HG, OB, G,
    TS, TR, TC, TY, TZ, TO, PW, DR, DS, GW, EP, ES, ER, FV,
    l_sem, w_s, w_r, t_s, t_r, u_s, u_r, b_s, b_r, h_s, h_r, c_s, c_r,
    tr_s, tr_r, ty_s, ty_r, tz_s, tz_r, o_s, o_r, d_s, d_r, e_s, e_r, g_s, g_r, f_sem,
):
    r, c, d = lax.axis_index("row"), lax.axis_index("col"), lax.axis_index("depth")
    zl, y, x, k = c // 4, c % 4, d // 2, d % 2
    z = 2 * r + zl

    def znb(delta):
        other = (z + delta + 8) % 8
        return (other // 2, (other % 2) * 4 + y, d)

    def ynb(delta):
        return (r, zl * 4 + (y + delta + 4) % 4, d)

    def xnb(delta):
        return (r, c, ((x + delta + 4) % 4) * 2 + k)

    def dnb(delta):
        return (r, c, (d + delta + 8) % 8)

    sib = (r, c, x * 2 + 1 - k)
    pair = (r, (1 - zl) * 4 + y, d)
    wraps_up = jnp.where(d == 7, 1, 0)
    wraps_down = jnp.where(d == 0, 1, 0)
    following = (r, zl * 4 + (y + wraps_up) % 4, (d + 1) % 8)
    previous = (r, zl * 4 + (y + 4 - wraps_down) % 4, (d + 7) % 8)

    def remote(src, dst, ssem, rsem, to):
        return pltpu.make_async_remote_copy(
            src_ref=src, dst_ref=dst, send_sem=ssem, recv_sem=rsem, device_id=to, device_id_type=MESH
        )

    sends = []

    def send(src, dst, ssem, rsem, to):
        copy = remote(src, dst, ssem, rsem, to)
        copy.start()
        sends.append(copy)

    def arrived(dst, rsem):
        remote(dst, dst, l_sem.at[0], rsem, sib).wait_recv()

    def each(start, stop, step):
        def body(at, carry):
            step(at)
            return carry

        lax.fori_loop(start, stop, body, 0)

    def lanes(at, width):
        return pl.ds(pl.multiple_of(at * width, width), width)

    barrier = pltpu.get_barrier_semaphore()
    partners = [dnb(delta) for delta in range(1, 8)]
    partners += [ynb(delta) for delta in range(1, 4)]
    partners += [znb(delta) for delta in (1, -1, 2, -2)]
    partners += [following, previous]
    for partner in partners:
        pl.semaphore_signal(barrier, inc=1, device_id=partner, device_id_type=MESH)
    locals_ = [
        pltpu.make_async_copy(tok_in, T.at[zl], l_sem.at[1]),
        pltpu.make_async_copy(w_in, W.at[y], l_sem.at[2]),
        pltpu.make_async_copy(up_in.at[:, lanes(zl, HALF)], U.at[zl], l_sem.at[3]),
    ]
    for copy in locals_:
        copy.start()
    pl.semaphore_wait(barrier, len(partners))

    for first, way, side in ((0, 1, 0), (1, -1, 1)):
        for part in (first, 1 - first):
            send(w_in.at[part], W.at[y, part], w_s.at[side, part], w_r.at[side, part], ynb(way))
    send(tok_in.at[pl.ds(0, 384)], T.at[zl, pl.ds(0, 384)], t_s.at[0], t_r.at[0], znb(-1))
    send(tok_in.at[pl.ds(384, 384)], T.at[zl, pl.ds(384, 384)], t_s.at[1], t_r.at[1], znb(1))
    send(up_in.at[:, lanes(1 - zl, HALF)], U.at[zl], u_s.at[0], u_r.at[0], pair)
    for copy in locals_:
        copy.wait()
    spread = lax.dot_general(
        taps_ref[...], group_of_channel(0), (((1,), (0,)), ((), ())), precision=lax.Precision.HIGHEST,
        preferred_element_type=F32,
    )
    for at in range(8):
        SP[at, pl.ds(0, KT)] = spread[:, at * CH : (at + 1) * CH]

    def shard_at(i):
        return (y + (i * (7 - i)) // 2) % 4

    def unit(u):
        return (u + zl) % 2, shard_at(u // 2), 1 - 2 * (u % 2)

    def to_sibling(g, j):
        return remote(PP.at[g, j, :, 1 - k], SB.at[g, j], b_s.at[0, g, j], b_r.at[0, g, j], sib)

    def far(g, j, way):
        return remote(S.at[g, j, (x + 2) % 4], R2.at[g, j], b_s.at[1, g, j], b_r.at[1, g, j], xnb(way))

    def back(g, j, way):
        return remote(
            S.at[g, j, (x - way + 4) % 4], RM.at[g, j], b_s.at[2, g, j], b_r.at[2, g, j], xnb(-way)
        )

    def near(g, j, way):
        return remote(
            S.at[g, j, (x + way + 4) % 4], RP.at[g, j], b_s.at[3, g, j], b_r.at[3, g, j], xnb(way)
        )

    def project(u):
        g, j, _ = unit(u)
        part = fma_dot(T[g], W[j].reshape(SH, DL), ((1,), (1,)))
        PP[g, j] = part.astype(BF16).reshape(4, 2, ROWS, SH)
        to_sibling(g, j).start()

    def chip_sum(u):
        g, j, way = unit(u)
        to_sibling(g, j).wait_recv()
        for at in range(4):
            S[g, j, at] = (PP[g, j, at, k].astype(F32) + SB[g, j, at].astype(F32)).astype(BF16)
        far(g, j, way).start()
        back(g, j, way).start()

    def relay(u):
        g, j, way = unit(u)
        far(g, j, way).wait_recv()
        at = (x + way + 4) % 4
        S[g, j, at] = (S[g, j, at].astype(F32) + R2[g, j].astype(F32)).astype(BF16)
        near(g, j, way).start()

    def relayed_weights(part):
        way = 1 - 2 * part
        rows = W.at[(y - way + 4) % 4, part]
        return remote(rows, rows, w_s.at[2, part], w_r.at[2, part], ynb(way))

    def project_step(u):
        @pl.when(u == 1)
        def _():
            chip_sum(0)
            arrived(W.at[(y + 3) % 4, 0], w_r.at[0, 0])
            relayed_weights(0).start()
            arrived(W.at[(y + 1) % 4, 1], w_r.at[1, 1])
            relayed_weights(1).start()
            relay(0)
            arrived(T.at[1 - zl, pl.ds(0, 384)], t_r.at[0])
            arrived(T.at[1 - zl, pl.ds(384, 384)], t_r.at[1])

        @pl.when(u == 2)
        def _():
            arrived(W.at[(y + 3) % 4, 1], w_r.at[0, 1])

        @pl.when(u == 4)
        def _():
            arrived(W.at[(y + 1) % 4, 0], w_r.at[1, 0])

        @pl.when(u == 6)
        def _():
            chip_sum(5)
            arrived(W.at[(y + 2) % 4, 0], w_r.at[2, 0])
            arrived(W.at[(y + 2) % 4, 1], w_r.at[2, 1])

        project(u)

        @pl.when((u >= 2) & (u != 6))
        def _():
            chip_sum(u - 1)

        @pl.when(u >= 5)
        def _():
            relay(u - 4)

    each(0, 8, project_step)
    chip_sum(7)
    relay(4)
    relay(5)

    def mixed_rows(j):
        return remote(MX.at[j, :, pl.ds(ROWS, 8)], HM.at[j], h_s.at[0, j], h_r.at[0, j], following)

    def grad_rows(j):
        return remote(GF.at[j, :, pl.ds(0, 8)], HG.at[j], h_s.at[1, j], h_r.at[1, j], previous)

    def total_step(i):
        for half in range(2):
            g, j, way = unit(2 * i + half)
            back(g, j, way).wait_recv()
            near(g, j, way).wait_recv()
            total = S[g, j, x].astype(F32) + RM[g, j].astype(F32) + RP[g, j].astype(F32)
            total = total.astype(BF16).astype(F32)
            up = U[g, :, lanes(j, CH)].astype(F32)
            QKV[g, j] = total
            MX[j, g, pl.ds(8, ROWS)] = total[:, CH : 2 * CH] * total[:, 2 * CH :]
            GF[j, g, pl.ds(0, ROWS)] = up * total[:, :CH]
        mixed_rows(j).start()
        grad_rows(j).start()

    arrived(U.at[1 - zl], u_r.at[0])
    each(0, 3, total_step)
    each(6, 8, relay)
    each(3, 4, total_step)

    def own_piece(g, j, to_left):
        rows = G.at[g, x, k, :, lanes(j, SH)]
        return remote(rows, rows, c_s.at[to_left, g, j], c_r.at[to_left, g, j], xnb(1 - 2 * to_left))

    def relayed_piece(g, j, to_left):
        way = 1 - 2 * to_left
        rows = G.at[g, (x - way + 4) % 4, k, :, lanes(j, SH)]
        return remote(rows, rows, c_s.at[2, g, j], c_r.at[2, g, j], xnb(way))

    def to_sibling_back(g, j):
        rows = G.at[g, :, k, :, lanes(j, SH)]
        return remote(rows, rows, c_s.at[3, g, j], c_r.at[3, g, j], sib)

    def filter_step(g, i):
        j = shard_at(i)
        if g == 0:
            mixed_rows(j).wait_recv()
            grad_rows(j).wait_recv()
        at_start = (y == 0) & (d == 0)
        at_end = (y == 3) & (d == 7)
        same = jnp.where(at_start, 0.0, 1.0)
        swapped = jnp.where(at_start, 1.0 * g, 0.0)
        MX[j, g, pl.ds(0, 8)] = HM[j, g] * same + HM[j, 1 - g] * swapped
        same = jnp.where(at_end, 0.0, 1.0)
        swapped = jnp.where(at_end, 1.0 - g, 0.0)
        GF[j, g, pl.ds(ROWS, 8)] = HG[j, g] * same + HG[j, 1 - g] * swapped
        taps = SP[zl * 4 + j]
        query = QKV[g, j, :, :CH]
        up = U[g, :, lanes(j, CH)].astype(F32)
        grad = GF[j, g, pl.ds(0, ROWS)]
        filtered = jnp.zeros((ROWS, CH), F32)
        grad_mixed = jnp.zeros((ROWS, CH), F32)
        tap_sums = []
        for o in range(KT):
            shifted = MX[j, g, pl.ds(8 - o, ROWS)]
            tap = taps[o : o + 1]
            filtered = filtered + tap * shifted
            grad_mixed = grad_mixed + tap * GF[j, g, pl.ds(o, ROWS)]
            tap_sums.append(jnp.sum(grad * shifted, axis=0, keepdims=True))
        OB[g, :, lanes(j, CH)] = (query * filtered).astype(BF16)
        G[g, x, k, :, lanes(3 * j, CH)] = (up * filtered).astype(BF16)
        G[g, x, k, :, lanes(3 * j + 1, CH)] = (grad_mixed * QKV[g, j, :, 2 * CH :]).astype(BF16)
        G[g, x, k, :, lanes(3 * j + 2, CH)] = (grad_mixed * QKV[g, j, :, CH : 2 * CH]).astype(BF16)
        TS[g, j] = jnp.concatenate(tap_sums + [jnp.zeros((1, CH), F32)], axis=0)

        if g == 0:
            own_piece(g, j, 0).start()
            own_piece(g, j, 1).start()

    def relay_piece(g, i):
        j, to_left = shard_at(i), i % 2
        own_piece(g, j, to_left).wait_recv()
        relayed_piece(g, j, to_left).start()

    def sibling_piece(g, i):
        j, to_left = shard_at(i), i % 2
        own_piece(g, j, 1 - to_left).wait_recv()
        relayed_piece(g, j, to_left).wait_recv()
        to_sibling_back(g, j).start()

    def gathered(g, i):
        to_sibling_back(g, shard_at(i)).wait_recv()

    def second_group(i):
        filter_step(1, i)
        sibling_piece(0, i)
        own_piece(1, shard_at(i), 0).start()
        own_piece(1, shard_at(i), 1).start()

    each(0, 4, lambda i: filter_step(0, i))
    each(0, 4, lambda i: relay_piece(0, i))
    each(0, 4, second_group)
    send(OB.at[1 - zl], out_ref.at[:, lanes(zl, HALF)], o_s.at[0], o_r.at[0], pair)
    out_copy = pltpu.make_async_copy(OB.at[zl], out_ref.at[:, lanes(zl, HALF)], l_sem.at[4])
    out_copy.start()
    TC[...] = TS[0] + TS[1]
    for delta in range(1, 8):
        send(TC, TR.at[d], tr_s.at[delta], tr_r.at[d], dnb(delta))
    TR[d] = TC[...]

    def own_chunk(g, delta, piece):
        return EP[g, piece, lanes(((z + delta + 8) % 8) // 2, 2 * ROWS)]

    def chunk_copy(way, steps, piece):
        return remote(
            ES.at[way, steps, piece], ER.at[way, steps, piece],
            e_s.at[way, steps, piece], e_r.at[way, steps, piece], znb(1 - 2 * way),
        )

    def landed_chunk(way, steps, piece):
        chunk_copy(way, steps, piece).wait_recv()
        return ER[way, steps, piece].astype(F32)

    def send_chunk(g, way, steps, piece, received):
        value = own_chunk(g, steps * (1 - 2 * way), piece)
        if received:
            value = value + landed_chunk(way, steps + 1, piece)
        ES[way, steps, piece] = value.astype(BF16)
        chunk_copy(way, steps, piece).start()

    def shard_product(g, i, side):
        j = shard_at(i)
        rows = G[g, :, :, :, lanes(j, SH)].reshape(TOK, SH)
        return fma_dot(rows, W[j, :, :, lanes(side, HALF)].reshape(SH, HALF), ((1,), (0,)))

    def add_shard(g, i):
        gathered(g, i)
        for side in range(2):
            both = shard_product(g, i, side)
            for half in range(2):
                term = both[:, half * QUARTER : (half + 1) * QUARTER]
                if isinstance(i, int):
                    EP[g, 2 * side + half] = term
                else:
                    EP[g, 2 * side + half] += term

    def add_last_shard(g):
        gathered(g, 3)

        def step(side):
            both = shard_product(g, 3, side)
            EP[g, 2 * side] += both[:, :QUARTER]
            EP[g, 2 * side + 1] += both[:, QUARTER:]

            @pl.when((zl == g) & (side == 0))
            def _():
                send_chunk(g, 0, 4, 0, False)
                send_chunk(g, 0, 4, 1, False)

            @pl.when((zl == g) & (side == 1))
            def _():
                send_chunk(g, 1, 4, 3, False)
                send_chunk(g, 1, 4, 2, False)

            @pl.when((zl != g) & (side == 0))
            def _():
                send_chunk(g, 1, 3, 1, False)
                send_chunk(g, 1, 3, 0, False)

            @pl.when((zl != g) & (side == 1))
            def _():
                send_chunk(g, 0, 3, 2, False)
                send_chunk(g, 0, 3, 3, False)

        each(0, 2, step)

    def ring_step(g, owner, steps, start, stop):
        @pl.when((zl == g) == owner)
        def _():
            def step(at):
                piece = (at + 2) % 4
                send_chunk(g, 0, steps, piece, True)
                send_chunk(g, 1, steps, 3 - piece, True)

            each(start, stop, step)

    def final_rows(row, piece):
        return gt_ref.at[lanes((row + 4) % 4, 2 * ROWS), lanes(piece, QUARTER)]

    def final_copy(piece, way):
        return remote(
            FV.at[piece], final_rows(r, piece), g_s.at[way, piece], g_r.at[way, piece], znb(2 - 4 * way)
        )

    def final_relay(piece):
        way = piece % 2
        rows = final_rows(r - 1 + 2 * way, piece)
        return remote(rows, rows, g_s.at[2, piece], g_r.at[2, piece], znb(2 - 4 * way))

    def final_own(piece):
        return pltpu.make_async_copy(FV.at[piece], final_rows(r, piece), f_sem.at[piece])

    def finish(g, start, stop):
        @pl.when(zl == g)
        def _():
            def step(at):
                piece = (at + 2) % 4
                total = own_chunk(g, 0, piece) + landed_chunk(0, 1, piece) + landed_chunk(1, 1, piece)
                FV[piece] = total.astype(BF16)
                final_copy(piece, 0).start()
                final_copy(piece, 1).start()
                final_own(piece).start()

            each(start, stop, step)

    def finish_relay(g, start, stop):
        @pl.when(zl == g)
        def _():
            def step(at):
                piece = (at + 2) % 4
                way = piece % 2
                arrived(final_rows(r - 1 + 2 * way, piece), g_r.at[way, piece])
                final_relay(piece).start()

            each(start, stop, step)

    def shard_grad(delta):
        j = (y + delta + 4) % 4
        total = None
        for g in range(2):
            term = fma_dot(G[g, :, :, :, lanes(j, SH)].reshape(TOK, SH), T[g], ((0,), (0,)))
            total = term if total is None else total + term
        return total

    def send_grad(way, kind, value):
        DS[way, kind] = value.astype(BF16)
        send(DS.at[way, kind], DR.at[way, kind], d_s.at[way, kind], d_r.at[way, kind], ynb(1 - 2 * way))

    def landed_grad(way, kind):
        arrived(DR.at[way, kind], d_r.at[way, kind])
        return DR[way, kind].astype(F32)

    cut = SH // 2
    add_shard(0, 0)
    each(1, 3, lambda i: add_shard(0, i))
    each(0, 2, lambda i: relay_piece(1, i))
    add_last_shard(0)
    each(2, 4, lambda i: relay_piece(1, i))
    ring_step(0, False, 3, 2, 4)
    ring_step(0, True, 2, 0, 2)
    each(0, 4, lambda i: sibling_piece(1, i))
    add_shard(1, 0)
    ring_step(0, True, 2, 2, 4)
    each(1, 3, lambda i: add_shard(1, i))
    ring_step(0, False, 1, 0, 2)
    add_last_shard(1)
    ring_step(1, False, 3, 2, 4)
    ring_step(0, False, 1, 2, 4)
    part = shard_grad(2)
    send_grad(0, 0, part[:cut])
    send_grad(1, 0, part[cut:])
    ring_step(1, True, 2, 0, 2)
    ring_step(1, True, 2, 2, 4)
    ring_step(1, False, 1, 0, 2)
    ring_step(1, False, 1, 2, 4)
    finish(0, 0, 4)
    finish(1, 0, 4)
    part = shard_grad(1)
    send_grad(0, 1, part[cut:])
    PW[0] = part[:cut]
    part = shard_grad(-1)
    send_grad(1, 1, part[:cut])
    PW[1] = part[cut:]

    for delta in range(1, 8):
        source = (d + delta) % 8
        arrived(TR.at[source], tr_r.at[source])
    total = TR[0]
    for at in range(1, 8):
        total = total + TR[at]
    TZ[...] = total
    TY[y] = total
    for delta in range(1, 4):
        send(TZ, TY.at[y], ty_s.at[delta], ty_r.at[y], ynb(delta))

    send_grad(0, 2, PW[0] + landed_grad(0, 0))
    send_grad(1, 2, PW[1] + landed_grad(1, 0))
    finish_relay(0, 0, 4)
    finish_relay(1, 0, 4)
    GW[...] = shard_grad(0)

    for delta in range(1, 4):
        source = (y + delta) % 4
        arrived(TY.at[source], ty_r.at[source])
    total = TY[0]
    for at in range(1, 4):
        total = total + TY[at]
    TO[zl] = total
    send(TO.at[zl], TO.at[zl], tz_s.at[0], tz_r.at[0], pair)

    GW[pl.ds(0, cut)] = GW[pl.ds(0, cut)] + landed_grad(0, 2) + landed_grad(1, 1)
    GW[pl.ds(cut, cut)] = GW[pl.ds(cut, cut)] + landed_grad(0, 1) + landed_grad(1, 2)
    gw_copy = pltpu.make_async_copy(GW, gw_ref, l_sem.at[5])
    gw_copy.start()

    arrived(TO.at[1 - zl], tz_r.at[0])
    sums = jnp.concatenate([TO[at // 4, at % 4] for at in range(8)], axis=1)
    ts_ref[...] = lax.dot_general(
        sums, group_of_channel(1), (((1,), (0,)), ((), ())), precision=lax.Precision.HIGHEST,
        preferred_element_type=F32,
    )[:KT]
    arrived(out_ref.at[:, lanes(1 - zl, HALF)], o_r.at[0])
    for piece in range(4):
        way = piece % 2
        arrived(final_rows(r + 1 - 2 * way, piece), g_r.at[1 - way, piece])
        arrived(final_rows(r + 2, piece), g_r.at[2, piece])
        final_own(piece).wait()
    out_copy.wait()
    gw_copy.wait()

    for copy in sends:
        copy.wait_send()
    for part in range(2):
        relayed_weights(part).wait_send()

    def sent_piece(piece):
        final_relay(piece).wait_send()
        for way in range(2):
            final_copy(piece, way).wait_send()
            for steps in range(1, 4):
                chunk_copy(way, steps, piece).wait_send()
        chunk_copy(piece // 2, 4, piece).wait_send()

    each(0, 4, sent_piece)

    def sent_step(u):
        g, j, way = unit(u)

        @pl.when(u % 2 == 0)
        def _():
            mixed_rows(j).wait_send()
            grad_rows(j).wait_send()

        for copy in (to_sibling(g, j), far(g, j, way), back(g, j, way), near(g, j, way)):
            copy.wait_send()
        for copy in (
            own_piece(g, j, 0), own_piece(g, j, 1), relayed_piece(g, j, (u // 2) % 2), to_sibling_back(g, j)
        ):
            copy.wait_send()

    each(0, 8, sent_step)


def hand_over(out_in, gt_in, gw_in, taps_in, out_ref, gt_ref, gw_ref, taps_ref, out_v, gt_v, gw_v, sem):
    steps = []
    for src, held, dst, parts in ((gt_in, gt_v, gt_ref, 4), (gw_in, gw_v, gw_ref, 4), (out_in, out_v, out_ref, 1)):
        rows = held.shape[0] // parts
        for part in range(parts):
            at = pl.ds(part * rows, rows)
            steps.append((src.at[at], held.at[at], dst.at[at]))
    reads = [pltpu.make_async_copy(src, held, sem.at[0, n]) for n, (src, held, _) in enumerate(steps)]
    writes = [pltpu.make_async_copy(held, dst, sem.at[1, n]) for n, (_, held, dst) in enumerate(steps)]
    for copy in reads:
        copy.start()
    taps_ref[...] = taps_in[...]
    for read, write in zip(reads, writes):
        read.wait()
        write.start()
    for copy in writes:
        copy.wait()


def on_device(tokens, weight, taps, upstream):
    shard = weight.transpose(1, 0, 2).reshape(2, SH // 2, DL)
    vmem = pl.BlockSpec(memory_space=pltpu.VMEM)
    anywhere = pl.BlockSpec(memory_space=pl.ANY)
    dma = pltpu.SemaphoreType.DMA
    scratch = [
        pltpu.VMEM((2, TOK, DL), BF16),
        pltpu.VMEM((4, 2, SH // 2, DL), BF16),
        pltpu.VMEM((8, 8, CH), F32),
        pltpu.VMEM((2, ROWS, HALF), BF16),
        pltpu.VMEM((2, 4, 4, 2, ROWS, SH), BF16),
        pltpu.VMEM((2, 4, 4, ROWS, SH), BF16),
        pltpu.VMEM((2, 4, 4, ROWS, SH), BF16),
        pltpu.VMEM((2, 4, ROWS, SH), BF16),
        pltpu.VMEM((2, 4, ROWS, SH), BF16),
        pltpu.VMEM((2, 4, ROWS, SH), BF16),
        pltpu.VMEM((2, 4, ROWS, SH), F32),
        pltpu.VMEM((4, 2, ROWS + 8, CH), F32),
        pltpu.VMEM((4, 2, ROWS + 8, CH), F32),
        pltpu.VMEM((4, 2, 8, CH), F32),
        pltpu.VMEM((4, 2, 8, CH), F32),
        pltpu.VMEM((2, ROWS, HALF), BF16),
        pltpu.VMEM((2, 4, 2, ROWS, 4 * SH), BF16),
        pltpu.VMEM((2, 4, 8, CH), F32),
        pltpu.VMEM((8, 4, 8, CH), F32),
        pltpu.VMEM((4, 8, CH), F32),
        pltpu.VMEM((4, 4, 8, CH), F32),
        pltpu.VMEM((4, 8, CH), F32),
        pltpu.VMEM((2, 4, 8, CH), F32),
        pltpu.VMEM((2, SH // 2, DL), F32),
        pltpu.VMEM((2, 3, SH // 2, DL), BF16),
        pltpu.VMEM((2, 3, SH // 2, DL), BF16),
        pltpu.VMEM((SH, DL), F32),
        pltpu.VMEM((2, 4, TOK, QUARTER), F32),
        pltpu.VMEM((2, 5, 4, 2 * ROWS, QUARTER), BF16),
        pltpu.VMEM((2, 5, 4, 2 * ROWS, QUARTER), BF16),
        pltpu.VMEM((4, 2 * ROWS, QUARTER), BF16),
        dma((6,)),
        dma((3, 2)), dma((3, 2)),
        dma((2,)), dma((2,)),
        dma((1,)), dma((1,)),
        dma((4, 2, 4)), dma((4, 2, 4)),
        dma((2, 4)), dma((2, 4)),
        dma((4, 2, 4)), dma((4, 2, 4)),
        dma((8,)), dma((8,)),
        dma((4,)), dma((4,)),
        dma((1,)), dma((1,)),
        dma((1,)), dma((1,)),
        dma((2, 3)), dma((2, 3)),
        dma((2, 5, 4)), dma((2, 5, 4)),
        dma((3, 4)), dma((3, 4)),
        dma((4,)),
    ]
    shapes = (
        jax.ShapeDtypeStruct((ROWS, 2 * HALF), BF16),
        jax.ShapeDtypeStruct((TOK, DL), BF16),
        jax.ShapeDtypeStruct((SH, DL), F32),
        jax.ShapeDtypeStruct((KT, 2 * HALF // GROUP), F32),
    )
    results = pl.pallas_call(
        kernel,
        out_shape=tuple(pltpu.VMEM(shape.shape, shape.dtype) for shape in shapes),
        in_specs=[anywhere, anywhere, vmem, anywhere],
        out_specs=(vmem, vmem, vmem, vmem),
        scratch_shapes=scratch,
        compiler_params=pltpu.CompilerParams(
            collective_id=0, has_side_effects=True, vmem_limit_bytes=58 * 1024 * 1024
        ),
        cost_estimate=pl.CostEstimate(
            flops=6 * TOK * DL * 8 * SH, bytes_accessed=8 * 1024 * 1024, transcendentals=0
        ),
    )(tokens, shard, taps, upstream)
    output, grad_tokens, grad_weight, grad_taps = results
    grad_weight = grad_weight.reshape(3, CH, DL).transpose(1, 0, 2)
    return output, grad_tokens, grad_weight, grad_taps


def solution(mesh):
    in_specs = (
        P("col", "depth"),
        P(("row", "col"), None, "depth"),
        P(None, "row"),
        P(("col", "depth"), "row"),
    )
    out_specs = (
        P(("col", "depth"), "row"),
        P("col", "depth"),
        P(("row", "col"), None, "depth"),
        P(None, "row"),
    )
    return jax.shard_map(
        on_device, mesh=mesh, in_specs=in_specs, out_specs=out_specs, check_vma=False
    )
```
